32 devices in a mesh: pipe: 2 (over core), ctx: 16 (over z, y, x).
Axes of the slice: x: 2, y: 2, z: 4, core: 2. Of those that a mesh axis runs over, the one named last changes fastest.
Arguments:
- saved: bfloat16 [2, 2048, 4096], P('pipe', 'ctx'), may hold values from -6 to 6
- grad_out: bfloat16 [2048, 4096], P('ctx'), may hold values from -6 to 6
- route_blocks: int32 [2, 16, 2], P('pipe', 'ctx'), may hold values from 0 to 31, as said below
- route_dest: int32 [2, 16, 2], P('pipe', 'ctx'), may hold values from -1 to 15, as said below
- gain: float32 [2, 4096], P('pipe'), may hold values from 0.5 to 2
- w_router: bfloat16 [2, 4096], P('pipe'), may hold values from -0.09375 to 0.09375
- w_gate: bfloat16 [2, 14336, 4096], P('pipe', 'ctx'), may hold values from -0.09375 to 0.09375
- w_up: bfloat16 [2, 14336, 4096], P('pipe', 'ctx'), may hold values from -0.09375 to 0.09375
- w_down: bfloat16 [2, 14336, 4096], P('pipe', 'ctx'), may hold values from -0.046875 to 0.046875
Outputs:
- grad_inputs: bfloat16 [2, 2048, 4096], P('pipe', 'ctx')
- grad_gate: float32 [2, 14336, 4096], P('pipe', 'ctx')
- grad_up: float32 [2, 14336, 4096], P('pipe', 'ctx')
- grad_down: float32 [2, 14336, 4096], P('pipe', 'ctx')
- grad_gain: float32 [2, 4096], P('pipe')
- grad_router: float32 [2, 4096], P('pipe')
The draws below stay inside these ranges and needn't reach their ends.
Inputs may be any that keep to these rules, and one draw needn't show every extreme that they name: In each row route_blocks[l, o, :] the 2 entries are distinct block numbers of owner o; only slots whose route_dest entry is not -1 are routed. In each row route_dest[l, o, :] the used slots come first: blocks that owner o works on itself (entry o), then blocks handed to the next owner (entry (o + 1) mod 16), then -1. An owner keeps at most 1 block and hands on at most 1; every device works on exactly 1 block of each layer, so 16 * 1 blocks are routed in each layer; in each layer some owner uses all 2 slots, keeping 1 and handing on 1.
All inputs are finite; a program needn't handle non-finite values.
Results may differ from the reference program's by a relative error of at most 0.007.
Values may be sent and summed in bfloat16 or wider, within the bound.
No kernel may reach another device: no remote copies, remote signals or barrier semaphores. Data moves between devices by JAX's collectives and lax.ppermute only.
A program may use at most 128 MiB of HBM per device.

```python
import math
import jax
import jax.numpy as jnp
from jax import lax

D = 4096
FF = 14336
BLOCK = 4
WORK = 1
TOK_DEV = 128
LAYERS = 2
BLK_DEV = 32
MOST = 2
TOKENS = 2048
N_CTX = 16


def draw_route_blocks(key, part):
    row_keys = jax.random.split(jax.random.fold_in(key, 11), LAYERS * N_CTX)

    def one_row(row_key):
        return jax.random.permutation(row_key, BLK_DEV)[:MOST]
    picked = jax.vmap(one_row)(row_keys)
    return picked.reshape(LAYERS, N_CTX, MOST).astype(jnp.int32)


def draw_route_dest(key, part):
    base_key = jax.random.fold_in(key, 23)
    keep_counts = jax.random.randint(jax.random.fold_in(base_key, 1), (LAYERS, N_CTX), 0, WORK + 1).astype(jnp.int32)
    heavy_owner = jax.random.randint(jax.random.fold_in(base_key, 2), (LAYERS, 1), 0, N_CTX).astype(jnp.int32)
    owners = jnp.arange(N_CTX, dtype=jnp.int32)[None, :]
    keep_counts = jnp.where(owners == heavy_owner, WORK, keep_counts)
    keep_counts = jnp.where(owners == (heavy_owner + 1) % N_CTX, 0, keep_counts)
    next_keep = jnp.roll(keep_counts, -1, axis=1)
    totals = keep_counts + WORK - next_keep
    slot_index = jnp.arange(MOST, dtype=jnp.int32)[None, None, :]
    owner_ids = jnp.broadcast_to(owners[:, :, None], (LAYERS, N_CTX, MOST))
    handed = jnp.where(slot_index < totals[:, :, None], (owner_ids + 1) % N_CTX, -1)
    targets = jnp.where(slot_index < keep_counts[:, :, None], owner_ids, handed)
    return targets.astype(jnp.int32)


def levels(key, dims, cuts, smallest, high):
    def one(dim, shards_of):
        heights = jax.random.uniform(jax.random.fold_in(jax.random.fold_in(key, 6), dim), (shards_of,), jnp.float32, smallest / len(cuts), high / len(cuts))
        return jnp.repeat(jnp.exp(heights), dims[dim] // shards_of).reshape((-1,) + (1,) * (len(dims) - dim - 1))

    factor_of = one(*cuts[0])
    for cut in cuts[1:]:
        factor_of = factor_of * one(*cut)
    return factor_of


def gaussian(rng, dims, deviation, limit, shards=(), kind=jnp.bfloat16):
    loudness = levels(rng, dims, shards, -0.22, 0.18) if shards else 1.0
    array = jax.random.normal(rng, dims, jnp.float32) * deviation * loudness
    return jnp.minimum(jnp.maximum(array, -limit), limit).astype(kind)


def setup_inputs(seed: int = 0) -> dict:
    key_of = jax.random.split(jax.random.key(seed), 10)
    saved = gaussian(key_of[0], (LAYERS, TOKENS, D), 1.0, 6.0, ((0, 2), (1, 16)))
    grad_out = gaussian(key_of[1], (TOKENS, D), 1.0, 6.0, ((0, 16),))
    route_blocks = draw_route_blocks(jax.random.fold_in(key_of[9], 71), 0)
    route_dest = draw_route_dest(jax.random.fold_in(key_of[9], 71), 0)
    gain = jnp.clip(jnp.exp(math.log(2.0) - 1.3862944 * jax.random.uniform(key_of[4], (LAYERS, D), jnp.float32) ** levels(key_of[4], (LAYERS, D), ((0, 2),), -0.2, 0.2)), 0.5, 2.0)
    w_router = gaussian(key_of[5], (LAYERS, D), D ** -0.5, 0.09375, ((0, 2),))
    w_gate = gaussian(key_of[6], (LAYERS, FF, D), D ** -0.5, 0.09375, ((0, 2), (1, 16)))
    w_up = gaussian(key_of[7], (LAYERS, FF, D), D ** -0.5, 0.09375, ((0, 2), (1, 16)))
    w_down = gaussian(key_of[8], (LAYERS, FF, D), FF ** -0.5, 0.046875, ((0, 2), (1, 16)))
    return {"saved": saved, "grad_out": grad_out, "route_blocks": route_blocks, "route_dest": route_dest, "gain": gain, "w_router": w_router, "w_gate": w_gate, "w_up": w_up, "w_down": w_down}


EPSILON = 1e-05

def silu_parts(gate_pre):
    sigma = jax.nn.sigmoid(gate_pre)
    return (gate_pre * sigma, sigma * (1.0 + gate_pre * (1.0 - sigma)))

def contract_last(left_side, right_side):
    return lax.dot_general(left_side, right_side, (((1,), (1,)), ((), ())), preferred_element_type=jnp.float32)

def contract_first(left_side, right_side):
    return lax.dot_general(left_side, right_side, (((0,), (0,)), ((), ())), preferred_element_type=jnp.float32)

def layer_backward(inputs, upstream, blocks, targets, gain_row, router_row, gate_weight, up_weight, down_weight):
    owner_ids = jnp.arange(N_CTX, dtype=jnp.int32)[:, None]
    starts = owner_ids * TOK_DEV + blocks.astype(jnp.int32) * BLOCK
    chosen = jnp.nonzero((targets >= 0).reshape(-1), size=N_CTX * WORK)[0].astype(jnp.int32)
    first_rows = starts.reshape(-1)[chosen]
    row_ids = (first_rows[:, None] + jnp.arange(BLOCK, dtype=jnp.int32)[None, :]).reshape(-1)
    picked = inputs[row_ids]
    picked_f = picked.astype(jnp.float32)
    inverse = lax.rsqrt(lax.optimization_barrier(jnp.mean(picked_f * picked_f, axis=1, keepdims=True)) + EPSILON)
    normal_hat = picked_f * inverse
    normed = (normal_hat * gain_row).astype(jnp.bfloat16)
    router_prob = jax.nn.sigmoid(jnp.dot(picked, router_row, preferred_element_type=jnp.float32))
    scaled = (router_prob[:, None] * upstream[row_ids].astype(jnp.float32)).astype(jnp.bfloat16)
    gate_pre = contract_last(normed, gate_weight)
    up_value = contract_last(normed, up_weight)
    activated, slope_term = silu_parts(gate_pre)
    hidden = (activated * up_value).astype(jnp.bfloat16)
    hidden_grad = contract_last(scaled, down_weight)
    row_sums = lax.optimization_barrier(jnp.sum(hidden_grad * hidden.astype(jnp.float32), axis=1))
    grad_down = contract_first(hidden, scaled)
    gate_grad = (hidden_grad * up_value * slope_term).astype(jnp.bfloat16)
    up_grad = (hidden_grad * activated).astype(jnp.bfloat16)
    grad_gate = contract_first(gate_grad, normed)
    grad_up = contract_first(up_grad, normed)
    normed_grad = jnp.dot(gate_grad, gate_weight, preferred_element_type=jnp.float32) + jnp.dot(up_grad, up_weight, preferred_element_type=jnp.float32)
    logit_grad = row_sums * (1.0 - router_prob)
    hat_grad = normed_grad * gain_row
    norm_part = inverse * (hat_grad - normal_hat * lax.optimization_barrier(jnp.mean(hat_grad * normal_hat, axis=1, keepdims=True)))
    row_delta = norm_part + logit_grad[:, None] * router_row.astype(jnp.float32)
    input_grad = upstream.astype(jnp.float32).at[row_ids].add(row_delta).astype(jnp.bfloat16)
    grad_gain = lax.optimization_barrier(jnp.sum(normed_grad * normal_hat, axis=0))
    grad_router = lax.optimization_barrier(jnp.sum(logit_grad[:, None] * picked_f, axis=0))
    return (input_grad, grad_gate, grad_up, grad_down, grad_gain, grad_router)

def reference(saved, grad_out, route_blocks, route_dest, gain, w_router, w_gate, w_up, w_down):
    upstream = grad_out
    results = [None] * LAYERS
    for layer_index in range(LAYERS - 1, -1, -1):
        results[layer_index] = layer_backward(saved[layer_index], upstream, route_blocks[layer_index], route_dest[layer_index], gain[layer_index], w_router[layer_index], w_gate[layer_index], w_up[layer_index], w_down[layer_index])
        upstream = results[layer_index][0]
    stacked = [jnp.stack([results[layer_index][position] for layer_index in range(LAYERS)]) for position in range(6)]
    return (stacked[0], stacked[1], stacked[2], stacked[3], stacked[4], stacked[5])
```

```python
import functools

import jax
import jax.numpy as jnp
from jax import lax
from jax.experimental import pallas as pl
from jax.experimental.pallas import tpu as pltpu
from jax.sharding import PartitionSpec as P

BLOCK = 4
EPSILON = 1e-05
LANES = 128
CHUNK = 512
GROUP = 16
VMEM_LIMIT = 48 * 1024 * 1024

F32 = jnp.float32
BF16 = jnp.bfloat16
VMEM_SPEC = pl.BlockSpec(memory_space=pltpu.VMEM)
SMEM_SPEC = pl.BlockSpec(memory_space=pltpu.SMEM)
ANY_SPEC = pl.BlockSpec(memory_space=pl.ANY)


def hop_order(peers):
    masks = []
    step = 1
    while step < peers:
        masks.append(step)
        step *= 2
    return masks[2:] + masks[:2][::-1]


def exchange(block, mask):
    peers = lax.axis_size("ctx")
    return lax.ppermute(block, "ctx", [(i, i ^ mask) for i in range(peers)])


def gather_all(block):
    held = block[None]
    for mask in hop_order(lax.axis_size("ctx")):
        held = jnp.concatenate([held, exchange(held, mask)], axis=0)
    return held


def scatter_sum(chunks, stats=None):
    for mask in hop_order(lax.axis_size("ctx"))[::-1]:
        half = chunks.shape[0] // 2
        sent = chunks[half:].astype(BF16)
        if stats is not None:
            high = lax.reduce_precision(stats, 8, 7)
            both = jnp.concatenate([high, stats - high], axis=0).astype(BF16)
            sent = jnp.concatenate([sent, both[None]], axis=0)
        received = exchange(sent, mask).astype(F32)
        chunks = chunks[:half] + received[:half]
        if stats is not None:
            rows = stats.shape[0]
            stats = stats + received[half, :rows] + received[half, rows:]
    return chunks[0], stats


def contract_last(left_side, right_side):
    return lax.dot_general(
        left_side, right_side, (((1,), (1,)), ((), ())), preferred_element_type=F32
    )


def pick_kernel(where_ref, saved_ref, grad_ref, keep_ref, hand_ref, groups, sems):
    model_dim = saved_ref.shape[1]
    blocks = (where_ref[0], where_ref[1])
    copies = []
    for slot in range(2):
        first = pl.multiple_of((blocks[slot] * BLOCK) // GROUP * GROUP, GROUP)
        for kind, source in enumerate((saved_ref, grad_ref)):
            copy = pltpu.make_async_copy(
                source.at[pl.ds(first, GROUP)], groups.at[slot, kind], sems.at[slot, kind]
            )
            copy.start()
            copies.append(copy)
    for copy in copies:
        copy.wait()
    rows = lax.broadcasted_iota(jnp.int32, (8, GROUP), 0)
    cols = lax.broadcasted_iota(jnp.int32, (8, GROUP), 1)
    lane = lax.broadcasted_iota(jnp.int32, (8, LANES), 1)
    for slot, out in enumerate((keep_ref, hand_ref)):
        offset = (blocks[slot] * BLOCK) % GROUP
        from_saved = jnp.where((rows < BLOCK) & (cols == offset + rows), 1.0, 0.0).astype(BF16)
        from_grad = jnp.where(
            (rows >= BLOCK) & (cols == offset + rows - BLOCK), 1.0, 0.0
        ).astype(BF16)
        for start in range(0, model_dim, CHUNK):
            at = slice(start, start + CHUNK)
            picked = jnp.dot(
                from_saved, groups[slot, 0, :, at], preferred_element_type=F32
            ) + jnp.dot(from_grad, groups[slot, 1, :, at], preferred_element_type=F32)
            out[:, at] = picked.astype(BF16)
        owner = where_ref[2].astype(F32)
        block = blocks[slot].astype(F32)
        flag = where_ref[3].astype(F32)
        out[:, model_dim:] = jnp.where(
            lane == 0, flag, jnp.where(lane == 1, owner, jnp.where(lane == 2, block, 0.0))
        ).astype(BF16)


def pick_blocks(where, saved, grad):
    model_dim = saved.shape[1]
    shape = jax.ShapeDtypeStruct((8, model_dim + LANES), BF16)
    return pl.pallas_call(
        pick_kernel,
        out_shape=(shape, shape),
        in_specs=[SMEM_SPEC, ANY_SPEC, ANY_SPEC],
        out_specs=(VMEM_SPEC, VMEM_SPEC),
        scratch_shapes=[
            pltpu.VMEM((2, 2, GROUP, model_dim), BF16),
            pltpu.SemaphoreType.DMA((2, 2)),
        ],
    )(where, saved, grad)


def layer_kernel(with_delta, tile, *refs):
    if with_delta:
        place_ref, pay_ref, gain_ref, router_ref, delta_ref, gate_hbm, up_hbm, down_hbm = refs[:8]
        refs = refs[8:]
    else:
        place_ref, pay_ref, gain_ref, router_ref, gate_hbm, up_hbm, down_hbm = refs[:7]
        refs = refs[7:]
    (hidden_ref, gate_grad_ref, up_grad_ref, scaled_ref, normed_ref, part_ref, stat_ref) = refs[:7]
    pair_w, down_w, picked_s, up_s, both_s, sem_g, sem_u, sem_d = refs[7:]
    half_pairs = pay_ref.shape[0]
    rows = half_pairs * 8
    model_dim = normed_ref.shape[1]
    ff_local = hidden_ref.shape[1]
    tiles = ff_local // tile
    middle = model_dim // 2

    copies = []
    for t in range(tiles):
        at = pl.ds(t * tile, tile)
        trio = (
            pltpu.make_async_copy(gate_hbm.at[at], pair_w.at[t, 0], sem_g.at[t]),
            pltpu.make_async_copy(up_hbm.at[at], pair_w.at[t, 1], sem_u.at[t]),
            pltpu.make_async_copy(down_hbm.at[at], down_w.at[t], sem_d.at[t]),
        )
        for copy in trio:
            copy.start()
        copies.append(trio)

    def split(start, width):
        even = pay_ref[:, 0, :, pl.ds(start, width)].astype(F32)
        odd = pay_ref[:, 1, :, pl.ds(start, width)].astype(F32)
        low = lax.broadcasted_iota(jnp.int32, even.shape, 1) < BLOCK
        first = jnp.where(low, even, pltpu.roll(odd, BLOCK, 1)).reshape(rows, width)
        second = jnp.where(low, pltpu.roll(even, BLOCK, 1), odd).reshape(rows, width)
        return first, second

    def gather_chunk(c, carry):
        squares, logits = carry
        start = pl.multiple_of(c * CHUNK, CHUNK)
        at = pl.ds(start, CHUNK)
        x, g = split(start, CHUNK)
        picked_s[:, at] = x.astype(BF16)
        up_s[:, at] = g.astype(BF16)
        squares = squares + jnp.sum(x * x, axis=1, keepdims=True)
        logits = logits + jnp.sum(x * router_ref[:, at].astype(F32), axis=1, keepdims=True)
        return squares, logits

    zero = jnp.zeros((rows, 1), F32)
    squares, logits = lax.fori_loop(0, model_dim // CHUNK, gather_chunk, (zero, zero))
    inverse = lax.rsqrt(squares * (1.0 / model_dim) + EPSILON)
    router = jax.nn.sigmoid(logits)

    if with_delta:
        own_meta, _ = split(model_dim, LANES)
        their_meta = delta_ref[:, :, middle:].astype(F32).reshape(rows * 2, LANES)
        lane_a = lax.broadcasted_iota(jnp.int32, (rows, LANES), 1)
        lane_b = lax.broadcasted_iota(jnp.int32, (rows * 2, LANES), 1)

        def difference(which):
            left = jnp.where(lane_a == which, own_meta, jnp.where(lane_a == 0, 1.0, 0.0))
            right = jnp.where(
                lane_b == which, 1.0, 0.0
            ) - jnp.where(lane_b == 0, jnp.sum(
                jnp.where(lane_b == which, their_meta, 0.0), axis=1, keepdims=True
            ), 0.0)
            return contract_last(left.astype(BF16), right.astype(BF16))

        same = (difference(1) == 0.0) & (difference(2) == 0.0) & (place_ref[0] == 0)
        row_a = lax.broadcasted_iota(jnp.int32, (rows, rows * 2), 0) % BLOCK
        row_b = lax.broadcasted_iota(jnp.int32, (rows, rows * 2), 1) % 8

    def scale_chunk(c, carry):
        start = pl.multiple_of(c * CHUNK, CHUNK)
        at = pl.ds(start, CHUNK)
        x = picked_s[:, at].astype(F32)
        normed_ref[:, at] = (x * inverse * gain_ref[:, at]).astype(BF16)
        upstream = up_s[:, at].astype(F32)
        if with_delta:
            second = jnp.where(start >= middle, 1, 0)
            chosen = jnp.where(same & (row_b == row_a + BLOCK * second), 1.0, 0.0).astype(BF16)
            from_at = pl.ds(pl.multiple_of(start - second * middle, CHUNK), CHUNK)
            deltas = delta_ref[:, :, from_at].astype(F32).reshape(rows * 2, CHUNK).astype(BF16)
            added = jnp.dot(chosen, deltas, preferred_element_type=F32)
            upstream = (upstream + added).astype(BF16).astype(F32)
        scaled_ref[:, at] = (router * upstream).astype(BF16)
        return carry

    lax.fori_loop(0, model_dim // CHUNK, scale_chunk, 0)

    row_sums = zero
    for t in range(tiles):
        for copy in copies[t]:
            copy.wait()
        pair = pair_w[t].reshape(2 * tile, model_dim)
        products = contract_last(normed_ref[...], pair)
        gate = products[:, :tile]
        up = products[:, tile:]
        hidden_grad = contract_last(scaled_ref[...], down_w[t])
        sigma = jax.nn.sigmoid(gate)
        activated = gate * sigma
        slope = sigma * (1.0 + gate * (1.0 - sigma))
        hidden = (activated * up).astype(BF16)
        gate_grad = (hidden_grad * up * slope).astype(BF16)
        up_grad = (hidden_grad * activated).astype(BF16)
        at = pl.ds(t * tile, tile)
        hidden_ref[:, at] = hidden
        gate_grad_ref[:, at] = gate_grad
        up_grad_ref[:, at] = up_grad
        both_s[t, :, :tile] = gate_grad
        both_s[t, :, tile:] = up_grad
        row_sums = row_sums + jnp.sum(hidden_grad * hidden.astype(F32), axis=1, keepdims=True)
    logit_part = row_sums * (1.0 - router)

    def out_chunk(c, carry):
        values = []
        for second in range(2):
            start = pl.multiple_of(c * CHUNK + second * middle, CHUNK)
            at = pl.ds(start, CHUNK)
            grad = jnp.zeros((rows, CHUNK), F32)
            for t in range(tiles):
                pair = pair_w[t, :, :, at].reshape(2 * tile, CHUNK)
                grad = grad + jnp.dot(both_s[t], pair, preferred_element_type=F32)
            x = picked_s[:, at].astype(F32)
            inner = pl.ds(pl.multiple_of(c * CHUNK, CHUNK), CHUNK)
            stat_ref[second : second + 1, inner] = jnp.sum(
                grad * (x * inverse), axis=0, keepdims=True
            )
            stat_ref[2 + second : 3 + second, inner] = jnp.sum(
                logit_part * x, axis=0, keepdims=True
            )
            values.append(grad.reshape(half_pairs, 8, CHUNK))
        a, b = values
        low = lax.broadcasted_iota(jnp.int32, a.shape, 1) < BLOCK
        at = pl.ds(pl.multiple_of(c * CHUNK, CHUNK), CHUNK)
        part_ref[:, 0, :, at] = jnp.where(low, a, pltpu.roll(b, BLOCK, 1))
        part_ref[:, 1, :, at] = jnp.where(low, pltpu.roll(a, BLOCK, 1), b)
        return carry

    lax.fori_loop(0, middle // CHUNK, out_chunk, 0)
    wide = jnp.broadcast_to(row_sums, (rows, LANES)).reshape(half_pairs, 8, LANES)
    part_ref[:, 0, :, middle:] = wide
    part_ref[:, 1, :, middle:] = pltpu.roll(wide, BLOCK, 1)
    stat_ref[:, middle:] = jnp.zeros((4, LANES), F32)


def layer_pass(place, pay, gain, router, gate_w, up_w, down_w, delta=None):
    peers = pay.shape[0]
    rows = peers * BLOCK
    ff_local, model_dim = gate_w.shape
    tile = LANES if ff_local % LANES == 0 else ff_local
    tiles = ff_local // tile
    wide = model_dim // 2 + LANES
    operands = [place, pay.reshape(peers // 2, 2, 8, model_dim + LANES), gain, router]
    in_specs = [SMEM_SPEC, VMEM_SPEC, VMEM_SPEC, VMEM_SPEC]
    if delta is not None:
        operands.append(delta)
        in_specs.append(VMEM_SPEC)
    operands += [gate_w, up_w, down_w]
    in_specs += [ANY_SPEC] * 3
    small = jax.ShapeDtypeStruct((rows, ff_local), BF16)
    large = jax.ShapeDtypeStruct((rows, model_dim), BF16)
    outs = pl.pallas_call(
        functools.partial(layer_kernel, delta is not None, tile),
        out_shape=(
            small,
            small,
            small,
            large,
            large,
            jax.ShapeDtypeStruct((peers // 2, 2, 8, wide), F32),
            jax.ShapeDtypeStruct((4, wide), F32),
        ),
        in_specs=in_specs,
        out_specs=(VMEM_SPEC,) * 7,
        scratch_shapes=[
            pltpu.VMEM((tiles, 2, tile, model_dim), BF16),
            pltpu.VMEM((tiles, tile, model_dim), BF16),
            pltpu.VMEM((rows, model_dim), BF16),
            pltpu.VMEM((rows, model_dim), BF16),
            pltpu.VMEM((tiles, rows, 2 * tile), BF16),
            pltpu.SemaphoreType.DMA((tiles,)),
            pltpu.SemaphoreType.DMA((tiles,)),
            pltpu.SemaphoreType.DMA((tiles,)),
        ],
        compiler_params=pltpu.CompilerParams(vmem_limit_bytes=VMEM_LIMIT),
        cost_estimate=pl.CostEstimate(
            flops=10 * rows * ff_local * model_dim,
            bytes_accessed=6 * ff_local * model_dim,
            transcendentals=rows * ff_local,
        ),
    )(*operands)
    hidden, gate_grad, up_grad, scaled, normed, part, stats = outs
    return hidden, gate_grad, up_grad, scaled, normed, part.reshape(peers, 8, wide), stats


def outer_kernel(left_ref, right_ref, out_ref):
    out_ref[...] = lax.dot_general(
        left_ref[...], right_ref[...], (((0,), (0,)), ((), ())), preferred_element_type=F32
    )


def weight_grad(left, right):
    rows, ff_local = left.shape
    model_dim = right.shape[1]
    tile = LANES if ff_local % LANES == 0 else ff_local
    return pl.pallas_call(
        outer_kernel,
        grid=(ff_local // tile,),
        out_shape=jax.ShapeDtypeStruct((ff_local, model_dim), F32),
        in_specs=[
            pl.BlockSpec((rows, tile), lambda t: (0, t)),
            pl.BlockSpec((rows, model_dim), lambda t: (0, 0)),
        ],
        out_specs=pl.BlockSpec((tile, model_dim), lambda t: (t, 0)),
        compiler_params=pltpu.CompilerParams(vmem_limit_bytes=24 * 1024 * 1024),
        cost_estimate=pl.CostEstimate(
            flops=2 * rows * ff_local * model_dim,
            bytes_accessed=4 * ff_local * model_dim,
            transcendentals=0,
        ),
    )(left, right)


def delta_kernel(pay_ref, sum_ref, gain_ref, router_ref, out_ref):
    middle = sum_ref.shape[1] - LANES
    x = pay_ref[...].astype(F32)[:BLOCK, : 2 * middle]
    sums = sum_ref[...]
    grad = jnp.concatenate([sums[:BLOCK, :middle], sums[BLOCK:, :middle]], axis=1)
    row_sum = sums[:BLOCK, middle : middle + 1]
    weight = router_ref[...].astype(F32)
    inverse = lax.rsqrt(jnp.mean(x * x, axis=1, keepdims=True) + EPSILON)
    hat = x * inverse
    router = jax.nn.sigmoid(jnp.sum(x * weight, axis=1, keepdims=True))
    hat_grad = grad * gain_ref[...]
    norm_part = inverse * (hat_grad - hat * jnp.mean(hat_grad * hat, axis=1, keepdims=True))
    delta = norm_part + row_sum * (1.0 - router) * weight
    out_ref[:, :middle] = jnp.concatenate([delta[:, :middle], delta[:, middle:]], axis=0).astype(
        BF16
    )
    out_ref[:, middle:] = pay_ref[:, 2 * middle :]


def delta_rows(pay, sums, gain, router):
    return pl.pallas_call(
        delta_kernel,
        out_shape=jax.ShapeDtypeStruct(sums.shape, BF16),
        in_specs=[VMEM_SPEC] * 4,
        out_specs=VMEM_SPEC,
    )(pay, sums, gain, router)


def add_kernel(place_ref, own_ref, other_ref, grad_ref, out_ref):
    middle = own_ref.shape[2] - LANES
    out_ref[...] = grad_ref[...]
    row = lax.broadcasted_iota(jnp.int32, (GROUP, 1), 0)
    first = place_ref[0] == 0

    def add(slot, base, deltas):
        block = place_ref[base]
        used = place_ref[base + 1]
        at = pl.ds(pl.multiple_of((block * BLOCK) // GROUP * GROUP, GROUP), GROUP)
        mask = (row // BLOCK == block % (GROUP // BLOCK)) & (used == 1)
        for half in range(2):
            cols = slice(half * middle, (half + 1) * middle)
            four = deltas[half * BLOCK : (half + 1) * BLOCK, :]
            spread = jnp.concatenate([four] * (GROUP // BLOCK), axis=0)
            out_ref[at, cols] = (
                out_ref[at, cols].astype(F32) + jnp.where(mask, spread, 0.0)
            ).astype(BF16)

    for slot in range(2):
        own = own_ref[slot, :, :middle].astype(F32)
        other = other_ref[slot, :, :middle].astype(F32)
        add(slot, 1 + 2 * slot, jnp.where(first, other, own))
    for slot in range(2):
        add(slot, 5 + 2 * slot, own_ref[slot, :, :middle].astype(F32))


def add_rows(place, own, other, grad):
    return pl.pallas_call(
        add_kernel,
        out_shape=jax.ShapeDtypeStruct(grad.shape, BF16),
        in_specs=[SMEM_SPEC] + [VMEM_SPEC] * 3,
        out_specs=VMEM_SPEC,
    )(place, own, other, grad)


def on_device(saved, grad_out, route_blocks, route_dest, gain, w_router, w_gate, w_up, w_down):
    section = lax.axis_index("pipe")
    me = lax.axis_index("ctx")
    sections = lax.axis_size("pipe")
    peers = lax.axis_size("ctx")
    tokens = saved[0]
    blocks = route_blocks[0, 0]
    targets = route_dest[0, 0]
    weights = (w_gate[0], w_up[0], w_down[0])

    routes = jnp.stack([blocks, targets])
    swap = [(i, sections - 1 - i) for i in range(sections)]
    other_routes = lax.ppermute(routes, "pipe", swap)

    def slots(table):
        kept = table[1, 0] == me
        handed_block = jnp.where(kept, table[0, 1], table[0, 0])
        handed = jnp.where(kept, table[1, 1], table[1, 0]) >= 0
        return table[0, 0], kept.astype(jnp.int32), handed_block, handed.astype(jnp.int32)

    mine = slots(routes)
    theirs = slots(other_routes)
    both_used = (routes[1] >= 0)[:, None] & (other_routes[1] >= 0)[None, :]
    shared = jnp.any((routes[0][:, None] == other_routes[0][None, :]) & both_used)
    where = jnp.stack([mine[0], mine[2], me.astype(jnp.int32), shared.astype(jnp.int32)])
    kept_rows, handed_rows = pick_blocks(where, tokens, grad_out)
    came = lax.ppermute(handed_rows, "ctx", [(i, (i + 1) % peers) for i in range(peers)])
    lane = lax.broadcasted_iota(jnp.int32, kept_rows.shape, 1)
    own_lane = lane == tokens.shape[1]
    pay_mine = jnp.where((mine[1] == 1) | own_lane, kept_rows, came)
    pay = gather_all(pay_mine)

    place = section.astype(jnp.int32)[None]
    run = functools.partial(layer_pass, place, pay, gain, w_router, *weights)
    state = run()

    def corrected(state):
        sums, _ = scatter_sum(state[5])
        delta = delta_rows(pay_mine, sums, gain, w_router)
        upper = lax.ppermute(delta, "pipe", swap)
        return run(gather_all(upper))

    any_shared = jnp.max(pay[:, 0, tokens.shape[1]].astype(F32)) > 0.5
    state = lax.cond(any_shared, corrected, lambda state: state, state)
    hidden, gate_grad, up_grad, scaled, normed, part, stats = state

    grad_down = weight_grad(hidden, scaled)
    grad_gate = weight_grad(gate_grad, normed)
    grad_up = weight_grad(up_grad, normed)
    sums, stats = scatter_sum(part, stats)
    delta = delta_rows(pay_mine, sums, gain, w_router)
    back = lax.ppermute(delta, "ctx", [(i, (i - 1) % peers) for i in range(peers)])
    own = jnp.stack([delta, back])
    other = lax.ppermute(own, "pipe", swap)
    last = section == sections - 1
    upper = [jnp.where(last, a, b) for a, b in zip(mine, theirs)]
    lower = [mine[0], jnp.where(last, 0, mine[1]), mine[2], jnp.where(last, 0, mine[3])]
    out_place = jnp.stack([section.astype(jnp.int32)] + upper + lower)
    grad_inputs = add_rows(out_place, own, other, grad_out)
    middle = tokens.shape[1] // 2
    return (
        grad_inputs[None],
        grad_gate[None],
        grad_up[None],
        grad_down[None],
        stats[:2, :middle].reshape(1, -1),
        stats[2:, :middle].reshape(1, -1),
    )


def solution(mesh):
    split = P("pipe", "ctx", None)
    row = P("pipe", None)
    return jax.shard_map(
        on_device,
        mesh=mesh,
        in_specs=(split, P("ctx", None), split, split, row, row, split, split, split),
        out_specs=(split, split, split, split, row, row),
        check_vma=False,
    )
```

```python
import functools

import jax
import jax.numpy as jnp
from jax import lax
from jax.experimental import pallas as pl
from jax.experimental.pallas import tpu as pltpu
from jax.sharding import PartitionSpec as P

BLOCK = 4
EPSILON = 1e-05
LANES = 128
CHUNK = 512
GROUP = 16
VMEM_LIMIT = 48 * 1024 * 1024

F32 = jnp.float32
BF16 = jnp.bfloat16
VMEM_SPEC = pl.BlockSpec(memory_space=pltpu.VMEM)
SMEM_SPEC = pl.BlockSpec(memory_space=pltpu.SMEM)
ANY_SPEC = pl.BlockSpec(memory_space=pl.ANY)


def hop_order(peers):
    masks = []
    step = 1
    while step < peers:
        masks.append(step)
        step *= 2
    return masks[2:] + masks[:2][::-1]


def exchange(block, mask):
    peers = lax.axis_size("ctx")
    return lax.ppermute(block, "ctx", [(i, i ^ mask) for i in range(peers)])


def gather_all(block):
    held = block[None]
    masks = hop_order(lax.axis_size("ctx"))
    for mask in masks[:-2]:
        held = jnp.concatenate([held, exchange(held, mask)], axis=0)
    near, far = masks[-2:]
    cut = (block.shape[1] - LANES) // 2
    first, second = held[:, :, :cut], held[:, :, cut:]
    count = held.shape[0]
    first_near = exchange(first, near)
    second_far = exchange(second, far)
    first = jnp.concatenate([first, first_near], axis=0)
    second_pair = jnp.concatenate([second, second_far], axis=0)
    first_far = exchange(first, far)
    second_near = exchange(second_pair, near)
    first = jnp.concatenate([first, first_far], axis=0)
    second = jnp.concatenate(
        [second, second_near[:count], second_far, second_near[count:]], axis=0
    )
    return first, second


def scatter_sum(chunks, stats, works):
    done = []
    for step, mask in enumerate(hop_order(lax.axis_size("ctx"))[::-1]):
        half = chunks.shape[0] // 2
        rows = stats.shape[0]
        high = lax.reduce_precision(stats, 8, 7)
        both = jnp.concatenate([high, stats - high], axis=0).astype(BF16)
        sent = jnp.concatenate([chunks[half:].astype(BF16), both[None]], axis=0)
        received = exchange(sent, mask)
        if step < len(works):
            left, right = works[step]
            left, _ = lax.optimization_barrier((left, sent))
            result = weight_grad(left, right)
            received, result = lax.optimization_barrier((received, result))
            done.append(result)
        received = received.astype(F32)
        chunks = chunks[:half] + received[:half]
        stats = stats + received[half, :rows] + received[half, rows:]
    return chunks[0], stats, done


def sum_all(rows):
    total = rows.astype(F32)
    for mask in hop_order(lax.axis_size("ctx")):
        total = total + exchange(total.astype(BF16), mask).astype(F32)
    return total


def contract_last(left_side, right_side):
    return lax.dot_general(
        left_side, right_side, (((1,), (1,)), ((), ())), preferred_element_type=F32
    )


def route_slots(blocks_ref, dest_ref, me):
    first, second = blocks_ref[0, 0, 0], blocks_ref[0, 0, 1]
    kept = dest_ref[0, 0, 0] == me
    handed = jnp.where(kept, dest_ref[0, 0, 1], dest_ref[0, 0, 0]) >= 0
    return (first, kept), (jnp.where(kept, second, first), handed)


def pick_kernel(
    here_ref, blocks_ref, dest_ref, other_blocks_ref, other_dest_ref, saved_ref, grad_ref,
    keep_ref, hand_ref, groups, sems,
):
    model_dim = saved_ref.shape[1]
    me = here_ref[1]
    slots = route_slots(blocks_ref, dest_ref, me)
    copies = []
    for slot, (block, _) in enumerate(slots):
        first = pl.multiple_of((block * BLOCK) // GROUP * GROUP, GROUP)
        for kind, source in enumerate((saved_ref, grad_ref)):
            copy = pltpu.make_async_copy(
                source.at[pl.ds(first, GROUP)], groups.at[slot, kind], sems.at[slot, kind]
            )
            copy.start()
            copies.append(copy)
    for copy in copies:
        copy.wait()
    rows = lax.broadcasted_iota(jnp.int32, (8, GROUP), 0)
    cols = lax.broadcasted_iota(jnp.int32, (8, GROUP), 1)
    lane = lax.broadcasted_iota(jnp.int32, (8, LANES), 1)
    for slot, out in enumerate((keep_ref, hand_ref)):
        block, used = slots[slot]
        offset = (block * BLOCK) % GROUP
        from_saved = jnp.where((rows < BLOCK) & (cols == offset + rows), 1.0, 0.0).astype(BF16)
        from_grad = jnp.where(
            (rows >= BLOCK) & (cols == offset + rows - BLOCK), 1.0, 0.0
        ).astype(BF16)
        for start in range(0, model_dim, CHUNK):
            at = slice(start, start + CHUNK)
            picked = jnp.dot(
                from_saved, groups[slot, 0, :, at], preferred_element_type=F32
            ) + jnp.dot(from_grad, groups[slot, 1, :, at], preferred_element_type=F32)
            out[:, at] = picked.astype(BF16)
        shared = jnp.int32(0)
        for j in range(2):
            same = (other_blocks_ref[0, 0, j] == block) & (other_dest_ref[0, 0, j] >= 0)
            shared = jnp.where(same & used, 1, shared)
        meta = jnp.zeros((8, LANES), F32)
        for index, value in enumerate((me, block, shared, used.astype(jnp.int32))):
            meta = jnp.where(lane == index, value.astype(F32), meta)
        out[:, model_dim:] = meta.astype(BF16)


def pick_blocks(here, routes, saved, grad):
    model_dim = saved.shape[1]
    shape = jax.ShapeDtypeStruct((8, model_dim + LANES), BF16)
    return pl.pallas_call(
        pick_kernel,
        out_shape=(shape, shape),
        in_specs=[SMEM_SPEC] * 5 + [ANY_SPEC, ANY_SPEC],
        out_specs=(VMEM_SPEC, VMEM_SPEC),
        scratch_shapes=[
            pltpu.VMEM((2, 2, GROUP, model_dim), BF16),
            pltpu.SemaphoreType.DMA((2, 2)),
        ],
    )(here, *routes, saved, grad)


def layer_kernel(with_delta, tile, *refs):
    if with_delta:
        delta_ref = refs[0]
        refs = refs[1:]
    here_ref, first_ref, second_ref, gain_ref, router_ref, gate_hbm, up_hbm, down_hbm = refs[:8]
    refs = refs[8:]
    (hidden_ref, gate_grad_ref, up_grad_ref, scaled_ref, normed_ref, part_ref, stat_ref) = refs[:7]
    if not with_delta:
        shared_part_ref, shared_x_ref = refs[7:9]
        refs = refs[2:]
    pair_w, down_w, picked_s, up_s, both_s, sem_g, sem_u, sem_d = refs[7:]
    half_pairs = first_ref.shape[0]
    rows = half_pairs * 8
    model_dim = normed_ref.shape[1]
    ff_local = hidden_ref.shape[1]
    tiles = ff_local // tile
    middle = model_dim // 2

    copies = []
    for t in range(tiles):
        at = pl.ds(t * tile, tile)
        trio = (
            pltpu.make_async_copy(gate_hbm.at[at], pair_w.at[t, 0], sem_g.at[t]),
            pltpu.make_async_copy(up_hbm.at[at], pair_w.at[t, 1], sem_u.at[t]),
            pltpu.make_async_copy(down_hbm.at[at], down_w.at[t], sem_d.at[t]),
        )
        for copy in trio:
            copy.start()
        copies.append(trio)

    def split(ref, start, width):
        even = ref[:, 0, :, pl.ds(start, width)].astype(F32)
        odd = ref[:, 1, :, pl.ds(start, width)].astype(F32)
        low = lax.broadcasted_iota(jnp.int32, even.shape, 1) < BLOCK
        first = jnp.where(low, even, pltpu.roll(odd, BLOCK, 1)).reshape(rows, width)
        second = jnp.where(low, pltpu.roll(even, BLOCK, 1), odd).reshape(rows, width)
        return first, second

    def gather_chunk(c, carry):
        squares, logits = carry
        inner = pl.multiple_of(c * CHUNK, CHUNK)
        for ref, base in ((first_ref, 0), (second_ref, middle)):
            at = pl.ds(pl.multiple_of(inner + base, CHUNK), CHUNK)
            x, g = split(ref, inner, CHUNK)
            picked_s[:, at] = x.astype(BF16)
            up_s[:, at] = g.astype(BF16)
            squares = squares + jnp.sum(x * x, axis=1, keepdims=True)
            logits = logits + jnp.sum(x * router_ref[:, at].astype(F32), axis=1, keepdims=True)
        return squares, logits

    zero = jnp.zeros((rows, 1), F32)
    squares, logits = lax.fori_loop(0, middle // CHUNK, gather_chunk, (zero, zero))
    inverse = lax.rsqrt(squares * (1.0 / model_dim) + EPSILON)
    router = jax.nn.sigmoid(logits)

    meta, _ = split(second_ref, middle, LANES)
    lane = lax.broadcasted_iota(jnp.int32, (8, LANES), 1)
    pick = lax.broadcasted_iota(jnp.int32, (8, LANES), 0) == lane
    across = contract_last(jnp.where(pick, 1.0, 0.0).astype(BF16), meta.astype(BF16))
    key_row = across[0:1] * LANES + across[1:2]
    key_col = meta[:, 0:1] * LANES + meta[:, 1:2]
    row_a = lax.broadcasted_iota(jnp.int32, (rows, rows), 0)
    row_b = lax.broadcasted_iota(jnp.int32, (rows, rows), 1)
    ahead = (key_col < key_row) & (meta[:, 2:3] > 0.5) & (row_a % BLOCK == 0)
    rank = jnp.sum(jnp.where(ahead, 1.0, 0.0), axis=0, keepdims=True)
    place = rank.astype(jnp.int32) * BLOCK + row_b % BLOCK
    chosen = jnp.where((place == row_a) & (across[2:3] > 0.5), 1.0, 0.0).astype(BF16)
    if with_delta:
        lower = jnp.where(here_ref[0] == 0, 1.0, 0.0).astype(BF16)
        spread = chosen[: delta_ref.shape[0]] * lower

    def scale_chunk(c, carry):
        at = pl.ds(pl.multiple_of(c * CHUNK, CHUNK), CHUNK)
        x = picked_s[:, at]
        normed_ref[:, at] = (x.astype(F32) * inverse * gain_ref[:, at]).astype(BF16)
        upstream = up_s[:, at].astype(F32)
        if with_delta:
            added = lax.dot_general(
                spread, delta_ref[:, at], (((0,), (0,)), ((), ())), preferred_element_type=F32
            )
            upstream = (upstream + added).astype(BF16).astype(F32)
        else:
            shared_x_ref[:, at] = jnp.dot(chosen, x, preferred_element_type=F32).astype(BF16)
        scaled_ref[:, at] = (router * upstream).astype(BF16)
        return carry

    lax.fori_loop(0, model_dim // CHUNK, scale_chunk, 0)

    row_sums = zero
    for t in range(tiles):
        for copy in copies[t]:
            copy.wait()
        pair = pair_w[t].reshape(2 * tile, model_dim)
        products = contract_last(normed_ref[...], pair)
        gate = products[:, :tile]
        up = products[:, tile:]
        hidden_grad = contract_last(scaled_ref[...], down_w[t])
        sigma = jax.nn.sigmoid(gate)
        activated = gate * sigma
        slope = sigma * (1.0 + gate * (1.0 - sigma))
        hidden = (activated * up).astype(BF16)
        gate_grad = (hidden_grad * up * slope).astype(BF16)
        up_grad = (hidden_grad * activated).astype(BF16)
        at = pl.ds(t * tile, tile)
        hidden_ref[:, at] = hidden
        gate_grad_ref[:, at] = gate_grad
        up_grad_ref[:, at] = up_grad
        both_s[t, :, :tile] = gate_grad
        both_s[t, :, tile:] = up_grad
        row_sums = row_sums + jnp.sum(hidden_grad * hidden.astype(F32), axis=1, keepdims=True)
    logit_part = row_sums * (1.0 - router)

    def out_chunk(c, carry):
        values = []
        for second in range(2):
            start = pl.multiple_of(c * CHUNK + second * middle, CHUNK)
            at = pl.ds(start, CHUNK)
            grad = jnp.zeros((rows, CHUNK), F32)
            for t in range(tiles):
                pair = pair_w[t, :, :, at].reshape(2 * tile, CHUNK)
                grad = grad + jnp.dot(both_s[t], pair, preferred_element_type=F32)
            x = picked_s[:, at].astype(F32)
            inner = pl.ds(pl.multiple_of(c * CHUNK, CHUNK), CHUNK)
            stat_ref[second : second + 1, inner] = jnp.sum(
                grad * (x * inverse), axis=0, keepdims=True
            )
            stat_ref[2 + second : 3 + second, inner] = jnp.sum(
                logit_part * x, axis=0, keepdims=True
            )
            if not with_delta:
                shared_part_ref[:, at] = jnp.dot(
                    chosen, grad.astype(BF16), preferred_element_type=F32
                ).astype(BF16)
            values.append(grad.reshape(half_pairs, 8, CHUNK))
        a, b = values
        low = lax.broadcasted_iota(jnp.int32, a.shape, 1) < BLOCK
        at = pl.ds(pl.multiple_of(c * CHUNK, CHUNK), CHUNK)
        part_ref[:, 0, :, at] = jnp.where(low, a, pltpu.roll(b, BLOCK, 1))
        part_ref[:, 1, :, at] = jnp.where(low, pltpu.roll(a, BLOCK, 1), b)
        return carry

    lax.fori_loop(0, middle // CHUNK, out_chunk, 0)
    wide = jnp.broadcast_to(row_sums, (rows, LANES))
    if not with_delta:
        shared_part_ref[:, model_dim:] = jnp.dot(
            chosen, wide.astype(BF16), preferred_element_type=F32
        ).astype(BF16)
    wide = wide.reshape(half_pairs, 8, LANES)
    part_ref[:, 0, :, middle:] = wide
    part_ref[:, 1, :, middle:] = pltpu.roll(wide, BLOCK, 1)
    stat_ref[:, middle:] = jnp.zeros((4, LANES), F32)


def layer_pass(here, pay, gain, router, gate_w, up_w, down_w, delta=None):
    peers = pay[0].shape[0]
    rows = peers * BLOCK
    ff_local, model_dim = gate_w.shape
    tile = LANES if ff_local % LANES == 0 else ff_local
    tiles = ff_local // tile
    wide = model_dim // 2 + LANES
    pairs = [part.reshape((peers // 2, 2) + part.shape[1:]) for part in pay]
    operands = [here, *pairs, gain, router, gate_w, up_w, down_w]
    in_specs = [SMEM_SPEC] + [VMEM_SPEC] * 4 + [ANY_SPEC] * 3
    small = jax.ShapeDtypeStruct((rows, ff_local), BF16)
    large = jax.ShapeDtypeStruct((rows, model_dim), BF16)
    out_shape = [
        small,
        small,
        small,
        large,
        large,
        jax.ShapeDtypeStruct((peers // 2, 2, 8, wide), F32),
        jax.ShapeDtypeStruct((4, wide), F32),
    ]
    if delta is None:
        out_shape += [jax.ShapeDtypeStruct((rows, model_dim + LANES), BF16), large]
    else:
        operands = [delta] + operands
        in_specs = [VMEM_SPEC] + in_specs
    outs = pl.pallas_call(
        functools.partial(layer_kernel, delta is not None, tile),
        out_shape=out_shape,
        in_specs=in_specs,
        out_specs=[VMEM_SPEC] * len(out_shape),
        scratch_shapes=[
            pltpu.VMEM((tiles, 2, tile, model_dim), BF16),
            pltpu.VMEM((tiles, tile, model_dim), BF16),
            pltpu.VMEM((rows, model_dim), BF16),
            pltpu.VMEM((rows, model_dim), BF16),
            pltpu.VMEM((tiles, rows, 2 * tile), BF16),
            pltpu.SemaphoreType.DMA((tiles,)),
            pltpu.SemaphoreType.DMA((tiles,)),
            pltpu.SemaphoreType.DMA((tiles,)),
        ],
        compiler_params=pltpu.CompilerParams(vmem_limit_bytes=VMEM_LIMIT),
        cost_estimate=pl.CostEstimate(
            flops=10 * rows * ff_local * model_dim,
            bytes_accessed=6 * ff_local * model_dim,
            transcendentals=rows * ff_local,
        ),
    )(*operands)
    return tuple(outs[:7]), tuple(outs[7:])


def outer_kernel(tile, left_ref, right_ref, out_ref, ring, sems):
    tiles = left_ref.shape[1] // tile
    depth = ring.shape[0]
    copies = []
    for t in range(tiles):
        slot = t % depth
        if t >= depth:
            copies[t - depth].wait()
        ring[slot] = lax.dot_general(
            left_ref[:, t * tile : (t + 1) * tile],
            right_ref[...],
            (((0,), (0,)), ((), ())),
            preferred_element_type=F32,
        )
        copy = pltpu.make_async_copy(
            ring.at[slot], out_ref.at[pl.ds(t * tile, tile)], sems.at[slot]
        )
        copy.start()
        copies.append(copy)
    for copy in copies[-depth:]:
        copy.wait()


def weight_grad(left, right):
    rows, ff_local = left.shape
    model_dim = right.shape[1]
    tile = LANES if ff_local % LANES == 0 else ff_local
    depth = min(4, ff_local // tile)
    return pl.pallas_call(
        functools.partial(outer_kernel, tile),
        out_shape=jax.ShapeDtypeStruct((ff_local, model_dim), F32),
        in_specs=[VMEM_SPEC, VMEM_SPEC],
        out_specs=ANY_SPEC,
        scratch_shapes=[
            pltpu.VMEM((depth, tile, model_dim), F32),
            pltpu.SemaphoreType.DMA((depth,)),
        ],
        compiler_params=pltpu.CompilerParams(vmem_limit_bytes=24 * 1024 * 1024),
        cost_estimate=pl.CostEstimate(
            flops=2 * rows * ff_local * model_dim,
            bytes_accessed=4 * ff_local * model_dim,
            transcendentals=0,
        ),
    )(left, right)


def norm_backward(x, grad, row_sum, gain, weight):
    inverse = lax.rsqrt(jnp.mean(x * x, axis=1, keepdims=True) + EPSILON)
    hat = x * inverse
    router = jax.nn.sigmoid(jnp.sum(x * weight, axis=1, keepdims=True))
    hat_grad = grad * gain
    norm_part = inverse * (hat_grad - hat * jnp.mean(hat_grad * hat, axis=1, keepdims=True))
    return norm_part + row_sum * (1.0 - router) * weight


def delta_kernel(pay_ref, sum_ref, gain_ref, router_ref, out_ref):
    middle = out_ref.shape[1]
    x = pay_ref[...].astype(F32)[:BLOCK, : 2 * middle]
    sums = sum_ref[...]
    grad = jnp.concatenate([sums[:BLOCK, :middle], sums[BLOCK:, :middle]], axis=1)
    row_sum = sums[:BLOCK, middle : middle + 1]
    delta = norm_backward(x, grad, row_sum, gain_ref[...], router_ref[...].astype(F32))
    out_ref[...] = jnp.concatenate([delta[:, :middle], delta[:, middle:]], axis=0).astype(BF16)


def delta_rows(pay, sums, gain, router):
    return pl.pallas_call(
        delta_kernel,
        out_shape=jax.ShapeDtypeStruct((8, sums.shape[1] - LANES), BF16),
        in_specs=[VMEM_SPEC] * 4,
        out_specs=VMEM_SPEC,
    )(pay, sums, gain, router)


def shared_kernel(x_ref, sum_ref, gain_ref, router_ref, out_ref):
    model_dim = x_ref.shape[1]
    delta = norm_backward(
        x_ref[...].astype(F32),
        sum_ref[:, :model_dim],
        sum_ref[:, model_dim : model_dim + 1],
        gain_ref[...],
        router_ref[...].astype(F32),
    )
    out_ref[...] = delta.astype(BF16)


def shared_rows(x, sums, gain, router):
    return pl.pallas_call(
        shared_kernel,
        out_shape=jax.ShapeDtypeStruct(x.shape, BF16),
        in_specs=[VMEM_SPEC] * 4,
        out_specs=VMEM_SPEC,
        compiler_params=pltpu.CompilerParams(vmem_limit_bytes=VMEM_LIMIT),
    )(x, sums, gain, router)


def add_kernel(
    here_ref, blocks_ref, dest_ref, other_blocks_ref, other_dest_ref,
    own_ref, back_ref, other_ref, other_back_ref, grad_ref, out_ref,
):
    middle = own_ref.shape[1]
    lower = here_ref[0] == 0
    mine = route_slots(blocks_ref, dest_ref, here_ref[1])
    theirs = route_slots(other_blocks_ref, other_dest_ref, here_ref[1])
    out_ref[...] = grad_ref[...]
    row = lax.broadcasted_iota(jnp.int32, (GROUP, 1), 0)

    def add(block, used, deltas):
        at = pl.ds(pl.multiple_of((block * BLOCK) // GROUP * GROUP, GROUP), GROUP)
        mask = (row // BLOCK == block % (GROUP // BLOCK)) & used
        for half in range(2):
            cols = slice(half * middle, (half + 1) * middle)
            four = deltas[half * BLOCK : (half + 1) * BLOCK, :]
            spread = jnp.concatenate([four] * (GROUP // BLOCK), axis=0)
            out_ref[at, cols] = (
                out_ref[at, cols].astype(F32) + jnp.where(mask, spread, 0.0)
            ).astype(BF16)

    for slot, (own, other) in enumerate(((own_ref, other_ref), (back_ref, other_back_ref))):
        block = jnp.where(lower, theirs[slot][0], mine[slot][0])
        used = jnp.where(lower, theirs[slot][1], mine[slot][1])
        deltas = jnp.where(lower, other[...].astype(F32), own[...].astype(F32))
        add(block, used, deltas)
    for slot, own in enumerate((own_ref, back_ref)):
        add(mine[slot][0], mine[slot][1] & lower, own[...].astype(F32))


def add_rows(here, routes, deltas, grad):
    return pl.pallas_call(
        add_kernel,
        out_shape=jax.ShapeDtypeStruct(grad.shape, BF16),
        in_specs=[SMEM_SPEC] * 5 + [VMEM_SPEC] * 5,
        out_specs=VMEM_SPEC,
    )(here, *routes, *deltas, grad)


def on_device(saved, grad_out, route_blocks, route_dest, gain, w_router, w_gate, w_up, w_down):
    sections = lax.axis_size("pipe")
    peers = lax.axis_size("ctx")
    here = jnp.stack([lax.axis_index("pipe"), lax.axis_index("ctx")]).astype(jnp.int32)
    tokens = saved[0]
    model_dim = tokens.shape[1]
    weights = (w_gate[0], w_up[0], w_down[0])

    swap = [(i, sections - 1 - i) for i in range(sections)]
    routes = (
        route_blocks,
        route_dest,
        lax.ppermute(route_blocks, "pipe", swap),
        lax.ppermute(route_dest, "pipe", swap),
    )
    kept_rows, handed_rows = pick_blocks(here, routes, tokens, grad_out)
    came = lax.ppermute(handed_rows, "ctx", [(i, (i + 1) % peers) for i in range(peers)])
    pay_mine = jnp.where(kept_rows[0, model_dim + 3] > 0.5, kept_rows, came)
    pay = gather_all(pay_mine)
    run = functools.partial(layer_pass, here, pay, gain, w_router, *weights)
    state, (shared_part, shared_x) = run()

    def corrected(count):
        def branch(state):
            sums = sum_all(shared_part[:count])
            upper = shared_rows(shared_x[:count], sums, gain, w_router)
            return run(delta=lax.ppermute(upper, "pipe", swap))[0]

        return branch

    few = 2
    shared = jnp.sum(pay[1][:, 0, model_dim // 2 + 2].astype(F32))
    case = (shared > 0.5).astype(jnp.int32) + (shared > few + 0.5).astype(jnp.int32)
    state = lax.switch(
        case, (lambda state: state, corrected(few * BLOCK), corrected(peers * BLOCK)), state
    )
    hidden, gate_grad, up_grad, scaled, normed, part, stats = state

    part = part.reshape((peers, 8, -1))
    works = ((hidden, scaled), (gate_grad, normed), (up_grad, normed))
    sums, stats, (grad_down, grad_gate, grad_up) = scatter_sum(part, stats, works)
    delta = delta_rows(pay_mine, sums, gain, w_router)
    back = lax.ppermute(delta, "ctx", [(i, (i - 1) % peers) for i in range(peers)])
    other = lax.ppermute(delta, "pipe", swap)
    other_back = lax.ppermute(back, "pipe", swap)
    grad_inputs = add_rows(here, routes, (delta, back, other, other_back), grad_out)
    middle = model_dim // 2
    return (
        grad_inputs[None],
        grad_gate[None],
        grad_up[None],
        grad_down[None],
        stats[:2, :middle].reshape(1, -1),
        stats[2:, :middle].reshape(1, -1),
    )


def solution(mesh):
    split = P("pipe", "ctx", None)
    row = P("pipe", None)
    return jax.shard_map(
        on_device,
        mesh=mesh,
        in_specs=(split, P("ctx", None), split, split, row, row, split, split, split),
        out_specs=(split, split, split, split, row, row),
        check_vma=False,
    )
```

```python
import functools

import jax
import jax.numpy as jnp
from jax import lax
from jax.experimental import pallas as pl
from jax.experimental.pallas import tpu as pltpu
from jax.sharding import PartitionSpec as P

BLOCK = 4
EPSILON = 1e-05
LANES = 128
CHUNK = 512
WIDE = 1024
SHARES = (7, 4, 4, 4, 2, 0)
GROUP = 16
TILE = 256
VMEM_LIMIT = 10 * 1024 * 1024
STREAM_LIMIT = 52 * 1024 * 1024
SMALL_LIMIT = 6 * 1024 * 1024

F32 = jnp.float32
BF16 = jnp.bfloat16
VMEM_SPEC = pl.BlockSpec(memory_space=pltpu.VMEM)
SMEM_SPEC = pl.BlockSpec(memory_space=pltpu.SMEM)
ANY_SPEC = pl.BlockSpec(memory_space=pl.ANY)
HBM_SPEC = pl.BlockSpec(memory_space=pltpu.HBM)


def hop_order(peers):
    masks = []
    step = 1
    while step < peers:
        masks.append(step)
        step *= 2
    return masks[2:] + masks[:2][::-1]


def exchange(block, mask):
    peers = lax.axis_size("ctx")
    return lax.ppermute(block, "ctx", [(i, i ^ mask) for i in range(peers)])


def first_pair(kept, handed, weight):
    peers = lax.axis_size("ctx")
    mask = hop_order(peers)[0]
    came = lax.ppermute(handed, "ctx", [(i, (i + 1) % peers) for i in range(peers)])
    far_kept = exchange(kept, mask)
    far_came = lax.ppermute(handed, "ctx", [(i, ((i + 1) % peers) ^ mask) for i in range(peers)])
    came, weight = beside(came, handed, weight)
    used = kept.shape[1] - LANES + 3
    mine = jnp.where(kept[:1, used : used + 1] > 0.5, kept, came)
    far = jnp.where(far_kept[:1, used : used + 1] > 0.5, far_kept, far_came)
    return mine, jnp.stack([mine, far]), weight


def gather_all(held, weights):
    masks = hop_order(lax.axis_size("ctx"))
    cut = (held.shape[2] - LANES) // 2
    up_w, down_w = weights
    for mask in masks[1:-2]:
        came = exchange(held, mask)
        if mask == masks[-3]:
            came, up_w = beside(came, held, up_w)
        held = jnp.concatenate([held, came], axis=0)
    near, far = masks[-2:]
    first, second = held[:, :, :cut], held[:, :, cut:]
    count = held.shape[0]
    first_near = exchange(first, near)
    second_far = exchange(second, far)
    second_far, down_w = beside(second_far, second, down_w)
    first = jnp.concatenate([first, first_near], axis=0)
    second_pair = jnp.concatenate([second, second_far], axis=0)
    first_far = exchange(first, far)
    second_near = exchange(second_pair, near)
    first = jnp.concatenate([first, first_far], axis=0)
    second = jnp.concatenate(
        [second, second_near[:count], second_far, second_near[count:]], axis=0
    )
    return (first, second), (up_w, down_w)


def scatter_sum(chunks, sent, stats, outers):
    rows = stats.shape[0]
    masks = hop_order(lax.axis_size("ctx"))[::-1]
    for step, mask in enumerate(masks):
        if step > 0:
            half = chunks.shape[0] // 2
            high = lax.reduce_precision(stats, 8, 7)
            both = jnp.concatenate([high, stats - high], axis=0).astype(BF16)
            sent = jnp.concatenate([chunks[half:].astype(BF16), both[None]], axis=0)
            chunks = chunks[:half]
        received = outers.beside(exchange(sent, mask), sent)
        if mask == masks[-1]:
            break
        received = received.astype(F32)
        half = chunks.shape[0]
        chunks = chunks + received[:half]
        stats = stats + received[half, :rows] + received[half, rows:]
    return chunks[0], stats, received


def sum_all(rows, weights):
    total = rows.astype(F32)
    fetched = []
    for mask in hop_order(lax.axis_size("ctx")):
        sent = total.astype(BF16)
        received = exchange(sent, mask)
        if len(fetched) < len(weights):
            received, weight = beside(received, sent, weights[len(fetched)])
            fetched.append(weight)
        total = total + received.astype(F32)
    return total, fetched


def contract_last(left_side, right_side):
    return lax.dot_general(
        left_side, right_side, (((1,), (1,)), ((), ())), preferred_element_type=F32
    )


def route_slots(blocks_ref, dest_ref, me):
    first, second = blocks_ref[0, 0, 0], blocks_ref[0, 0, 1]
    kept = dest_ref[0, 0, 0] == me
    handed = jnp.where(kept, dest_ref[0, 0, 1], dest_ref[0, 0, 0]) >= 0
    return (first, kept), (jnp.where(kept, second, first), handed)


def pick_kernel(
    here_ref, blocks_ref, dest_ref, other_blocks_ref, other_dest_ref, saved_ref, grad_ref,
    keep_ref, hand_ref, groups, sems,
):
    model_dim = saved_ref.shape[1]
    me = here_ref[1]
    slots = route_slots(blocks_ref, dest_ref, me)
    copies = []
    for slot, (block, _) in enumerate(slots):
        first = pl.multiple_of((block * BLOCK) // GROUP * GROUP, GROUP)
        for kind, source in enumerate((saved_ref, grad_ref)):
            copy = pltpu.make_async_copy(
                source.at[pl.ds(first, GROUP)], groups.at[slot, kind], sems.at[slot, kind]
            )
            copy.start()
            copies.append(copy)
    for copy in copies:
        copy.wait()
    rows = lax.broadcasted_iota(jnp.int32, (8, GROUP), 0)
    cols = lax.broadcasted_iota(jnp.int32, (8, GROUP), 1)
    lane = lax.broadcasted_iota(jnp.int32, (8, LANES), 1)
    for slot, out in enumerate((keep_ref, hand_ref)):
        block, used = slots[slot]
        offset = (block * BLOCK) % GROUP
        from_saved = jnp.where((rows < BLOCK) & (cols == offset + rows), 1.0, 0.0).astype(BF16)
        from_grad = jnp.where(
            (rows >= BLOCK) & (cols == offset + rows - BLOCK), 1.0, 0.0
        ).astype(BF16)
        for start in range(0, model_dim, CHUNK):
            at = slice(start, start + CHUNK)
            picked = jnp.dot(
                from_saved, groups[slot, 0, :, at], preferred_element_type=F32
            ) + jnp.dot(from_grad, groups[slot, 1, :, at], preferred_element_type=F32)
            out[:, at] = picked.astype(BF16)
        shared = jnp.int32(0)
        for j in range(2):
            same = (other_blocks_ref[0, 0, j] == block) & (other_dest_ref[0, 0, j] >= 0)
            shared = jnp.where(same & used, 1, shared)
        meta = jnp.zeros((8, LANES), F32)
        for index, value in enumerate((me, block, shared, used.astype(jnp.int32))):
            meta = jnp.where(lane == index, value.astype(F32), meta)
        out[:, model_dim:] = meta.astype(BF16)


def pick_blocks(here, routes, saved, grad):
    model_dim = saved.shape[1]
    shape = jax.ShapeDtypeStruct((8, model_dim + LANES), BF16)
    return pl.pallas_call(
        pick_kernel,
        out_shape=(shape, shape),
        in_specs=[SMEM_SPEC] * 5 + [ANY_SPEC, ANY_SPEC],
        out_specs=(VMEM_SPEC, VMEM_SPEC),
        scratch_shapes=[
            pltpu.VMEM((2, 2, GROUP, model_dim), BF16),
            pltpu.SemaphoreType.DMA((2, 2)),
        ],
        compiler_params=pltpu.CompilerParams(vmem_limit_bytes=SMALL_LIMIT),
    )(here, *routes, *(pltpu.with_memory_space_constraint(a, pltpu.HBM) for a in (saved, grad)))


def layer_kernel(with_delta, stream, tile, *refs):
    if with_delta:
        delta_ref, active_ref, up_slope_ref, hidden_ref = refs[:4]
        refs = refs[4:]
    here_ref, first_ref, second_ref, gain_ref, router_ref, gate_w, up_w, down_w = refs[:8]
    refs = refs[8:]
    gate_grad_ref, up_grad_ref, scaled_ref, keep_ref, sent_ref, stat_ref = refs[:6]
    refs = refs[6:]
    if not with_delta:
        hidden_ref, normed_ref, active_ref, up_slope_ref = refs[:4]
        shared_part_ref, shared_x_ref, case_ref = refs[4:7]
        refs = refs[7:]
    picked_s, up_s = refs[:2]
    waits = ()
    if stream:
        *held, sems = refs[2:]
        copies = [
            pltpu.make_async_copy(source, target, sems.at[index])
            for index, (source, target) in enumerate(zip((down_w, gate_w, up_w), held))
        ]
        for copy in copies:
            copy.start()
        down_w, gate_w, up_w = held
        waits = (copies[:1], copies[1:]) if with_delta else (copies, ())
    half_pairs = first_ref.shape[0]
    quarter = half_pairs // 2
    rows = half_pairs * 8
    model_dim = scaled_ref.shape[1]
    ff_local = gate_grad_ref.shape[1]
    middle = model_dim // 2

    def split(ref, start, width):
        even = ref[:, 0, :, pl.ds(start, width)].astype(F32)
        odd = ref[:, 1, :, pl.ds(start, width)].astype(F32)
        low = lax.broadcasted_iota(jnp.int32, even.shape, 1) < BLOCK
        first = jnp.where(low, even, pltpu.roll(odd, BLOCK, 1)).reshape(rows, width)
        second = jnp.where(low, pltpu.roll(even, BLOCK, 1), odd).reshape(rows, width)
        return first, second

    def gather_chunk(c, carry):
        squares, logits = carry
        inner = pl.multiple_of(c * WIDE, WIDE)
        for ref, base in ((first_ref, 0), (second_ref, middle)):
            at = pl.ds(pl.multiple_of(inner + base, WIDE), WIDE)
            x, g = split(ref, inner, WIDE)
            picked_s[:, at] = x.astype(BF16)
            up_s[:, at] = g.astype(BF16)
            squares = squares + jnp.sum(x * x, axis=1, keepdims=True)
            logits = logits + jnp.sum(x * router_ref[:, at].astype(F32), axis=1, keepdims=True)
        return squares, logits

    zero = jnp.zeros((rows, 1), F32)
    squares, logits = lax.fori_loop(0, middle // WIDE, gather_chunk, (zero, zero))
    inverse = lax.rsqrt(squares * (1.0 / model_dim) + EPSILON)
    router = jax.nn.sigmoid(logits)

    meta, _ = split(second_ref, middle, LANES)
    lane = lax.broadcasted_iota(jnp.int32, (8, LANES), 1)
    pick = lax.broadcasted_iota(jnp.int32, (8, LANES), 0) == lane
    across = contract_last(jnp.where(pick, 1.0, 0.0).astype(BF16), meta.astype(BF16))
    key_row = across[0:1] * LANES + across[1:2]
    key_col = meta[:, 0:1] * LANES + meta[:, 1:2]
    row_a = lax.broadcasted_iota(jnp.int32, (rows, rows), 0)
    row_b = lax.broadcasted_iota(jnp.int32, (rows, rows), 1)
    ahead = (key_col < key_row) & (meta[:, 2:3] > 0.5) & (row_a % BLOCK == 0)
    rank = jnp.sum(jnp.where(ahead, 1.0, 0.0), axis=0, keepdims=True)
    place = rank.astype(jnp.int32) * BLOCK + row_b % BLOCK
    chosen = jnp.where((place == row_a) & (across[2:3] > 0.5), 1.0, 0.0).astype(BF16)
    if with_delta:
        lower = jnp.where(here_ref[0] == 0, 1.0, 0.0).astype(BF16)
        spread = chosen[: delta_ref.shape[0]] * lower
    else:
        blocks = jnp.sum(across[2:3]) * (1.0 / BLOCK)
        few = shared_x_ref.shape[0] // BLOCK
        case_ref[0] = jnp.where(blocks > few + 0.5, 2, jnp.where(blocks > 0.5, 1, 0))
        chosen = chosen[: shared_x_ref.shape[0]]

    def scale_chunk(c, carry):
        at = pl.ds(pl.multiple_of(c * WIDE, WIDE), WIDE)
        x = picked_s[:, at]
        upstream = up_s[:, at].astype(F32)
        if with_delta:
            added = lax.dot_general(
                spread, delta_ref[:, at], (((0,), (0,)), ((), ())), preferred_element_type=F32
            )
            upstream = (upstream + added).astype(BF16).astype(F32)
        else:
            normed_ref[:, at] = (x.astype(F32) * inverse * gain_ref[:, at]).astype(BF16)
            shared_x_ref[:, at] = jnp.dot(chosen, x, preferred_element_type=F32).astype(BF16)
        scaled_ref[:, at] = (router * upstream).astype(BF16)
        return carry

    lax.fori_loop(0, model_dim // WIDE, scale_chunk, 0)

    row_sums = zero
    for copy in waits[0] if stream else ():
        copy.wait()
    for begin in range(0, ff_local, tile):
        at = slice(begin, min(begin + tile, ff_local))
        hidden_grad = contract_last(down_w[at, :], scaled_ref[...])
        if with_delta:
            activated = active_ref[at, :]
            up_slope = up_slope_ref[at, :]
        else:
            gate = contract_last(gate_w[at, :], normed_ref[...])
            up = contract_last(up_w[at, :], normed_ref[...])
            sigma = jax.nn.sigmoid(gate)
            activated = gate * sigma
            up_slope = up * (sigma * (1.0 + gate * (1.0 - sigma)))
            hidden = (activated * up).astype(BF16)
            hidden_ref[:, at] = hidden.T
            active_ref[at, :] = activated
            up_slope_ref[at, :] = up_slope
        gate_grad_ref[:, at] = (hidden_grad * up_slope).astype(BF16).T
        up_grad_ref[:, at] = (hidden_grad * activated).astype(BF16).T
        if with_delta:
            hidden = hidden_ref[:, at].T
        row_sums = row_sums + jnp.sum(hidden_grad * hidden.astype(F32), axis=0, keepdims=True).T
    logit_part = row_sums * (1.0 - router)

    low = lax.broadcasted_iota(jnp.int32, (half_pairs, 8, 1), 1) < BLOCK

    def store(even, odd, at):
        keep_ref[:, 0, :, at] = even[:quarter]
        keep_ref[:, 1, :, at] = odd[:quarter]
        for q in range(quarter):
            sent_ref[2 * q, :, at] = even[quarter + q].astype(BF16)
            sent_ref[2 * q + 1, :, at] = odd[quarter + q].astype(BF16)

    for copy in waits[1] if stream else ():
        copy.wait()

    def out_chunk(c, carry):
        at = pl.ds(pl.multiple_of(c * WIDE, WIDE), WIDE)
        halves = []
        gains = []
        routers = []
        for second in range(2):
            cols = pl.ds(pl.multiple_of(c * WIDE + second * middle, WIDE), WIDE)
            grad = jnp.dot(
                gate_grad_ref[...], gate_w[:, cols], preferred_element_type=F32
            ) + jnp.dot(up_grad_ref[...], up_w[:, cols], preferred_element_type=F32)
            x = picked_s[:, cols].astype(F32)
            gains.append(jnp.sum(grad * (x * inverse), axis=0, keepdims=True))
            routers.append(jnp.sum(logit_part * x, axis=0, keepdims=True))
            if not with_delta:
                shared_part_ref[:, cols] = jnp.dot(
                    chosen, grad.astype(BF16), preferred_element_type=F32
                ).astype(BF16)
            halves.append(grad.reshape(half_pairs, 8, WIDE))
        a, b = halves
        store(
            jnp.where(low, a, pltpu.roll(b, BLOCK, 1)),
            jnp.where(low, pltpu.roll(a, BLOCK, 1), b),
            at,
        )
        stats = jnp.concatenate(gains + routers, axis=0)
        high = stats.astype(BF16).astype(F32)
        stat_ref[:, at] = stats
        sent_ref[2 * quarter, :, at] = jnp.concatenate([high, stats - high], axis=0).astype(BF16)
        return carry

    lax.fori_loop(0, middle // WIDE, out_chunk, 0)
    wide = jnp.broadcast_to(row_sums, (rows, LANES))
    if not with_delta:
        shared_part_ref[:, model_dim:] = jnp.dot(
            chosen, wide.astype(BF16), preferred_element_type=F32
        ).astype(BF16)
    wide = wide.reshape(half_pairs, 8, LANES)
    store(wide, pltpu.roll(wide, BLOCK, 1), pl.ds(middle, LANES))
    stat_ref[:, middle:] = jnp.zeros((4, LANES), F32)
    sent_ref[2 * quarter, :, middle:] = jnp.zeros((8, LANES), BF16)


def fetch_kernel(source_ref, out_ref, sems):
    parts = sems.shape[0]
    size = source_ref.shape[0] // parts
    copies = []
    for part in range(parts):
        at = pl.ds(part * size, size)
        copy = pltpu.make_async_copy(source_ref.at[at], out_ref.at[at], sems.at[part])
        copy.start()
        copies.append(copy)
    for copy in copies:
        copy.wait()


def fetch(weight):
    return pl.pallas_call(
        fetch_kernel,
        out_shape=pltpu.VMEM(weight.shape, weight.dtype),
        in_specs=[HBM_SPEC],
        out_specs=VMEM_SPEC,
        scratch_shapes=[pltpu.SemaphoreType.DMA((7,))],
        compiler_params=pltpu.CompilerParams(vmem_limit_bytes=8 * 1024 * 1024),
        cost_estimate=pl.CostEstimate(
            flops=0, bytes_accessed=2 * weight.size, transcendentals=0
        ),
    )(pltpu.with_memory_space_constraint(weight, pltpu.HBM))


def beside(received, sent, weight):
    weight, _ = lax.optimization_barrier((weight, sent))
    fetched = fetch(weight)
    received, fetched = lax.optimization_barrier((received, fetched))
    return received, fetched


def layer_pass(here, pay, gain, router, weights, few, again=None, stream=False):
    peers = pay[0].shape[0]
    rows = peers * BLOCK
    ff_local, model_dim = weights[0].shape
    wide = model_dim // 2 + LANES
    pairs = [part.reshape((peers // 2, 2) + part.shape[1:]) for part in pay]
    if not stream:
        weights = [pltpu.with_memory_space_constraint(w, pltpu.VMEM) for w in weights]
    operands = [here, *pairs, gain, router, *weights]
    in_specs = [SMEM_SPEC] + [VMEM_SPEC] * 4 + [ANY_SPEC if stream else VMEM_SPEC] * 3
    scratch = [pltpu.VMEM((rows, model_dim), BF16)] * 2
    if stream:
        scratch += [pltpu.VMEM((ff_local, model_dim), BF16)] * 3
        scratch += [pltpu.SemaphoreType.DMA((3,))]
    small = jax.ShapeDtypeStruct((rows, ff_local), BF16)
    large = jax.ShapeDtypeStruct((rows, model_dim), BF16)
    tall = jax.ShapeDtypeStruct((ff_local, rows), F32)
    out_shape = [
        small,
        small,
        large,
        jax.ShapeDtypeStruct((peers // 4, 2, 8, wide), F32),
        jax.ShapeDtypeStruct((peers // 2 + 1, 8, wide), BF16),
        jax.ShapeDtypeStruct((4, wide), F32),
    ]
    out_specs = [VMEM_SPEC] * len(out_shape)
    if again is None:
        out_shape += [
            small,
            large,
            tall,
            tall,
            jax.ShapeDtypeStruct((few, model_dim + LANES), BF16),
            jax.ShapeDtypeStruct((few, model_dim), BF16),
            jax.ShapeDtypeStruct((1,), jnp.int32),
        ]
        out_specs += [VMEM_SPEC] * 6 + [SMEM_SPEC]
    else:
        operands = [*again, *operands]
        in_specs = [VMEM_SPEC] * len(again) + in_specs
    outs = pl.pallas_call(
        functools.partial(layer_kernel, again is not None, stream, TILE),
        out_shape=out_shape,
        in_specs=in_specs,
        out_specs=out_specs,
        scratch_shapes=scratch,
        compiler_params=pltpu.CompilerParams(
            vmem_limit_bytes=STREAM_LIMIT if stream else VMEM_LIMIT * max(1, rows // 64)
        ),
        cost_estimate=pl.CostEstimate(
            flops=10 * rows * ff_local * model_dim,
            bytes_accessed=6 * ff_local * model_dim,
            transcendentals=rows * ff_local,
        ),
    )(*operands)
    return tuple(outs[:6]), tuple(outs[6:])


def outer_kernel(tile, first, count, left_ref, right_ref, *refs):
    out_ref, ring, sems = refs[-3:]
    depth = ring.shape[0]
    copies = []
    for t in range(count):
        slot = t % depth
        if t >= depth:
            copies[t - depth].wait()
        ring[slot] = lax.dot_general(
            left_ref[:, (first + t) * tile : (first + t + 1) * tile],
            right_ref[...],
            (((0,), (0,)), ((), ())),
            preferred_element_type=F32,
        )
        copy = pltpu.make_async_copy(
            ring.at[slot], out_ref.at[pl.ds((first + t) * tile, tile)], sems.at[slot]
        )
        copy.start()
        copies.append(copy)
    for copy in copies[-depth:]:
        copy.wait()


def outer_tile(ff_local):
    return LANES if ff_local % LANES == 0 else ff_local


def weight_grad(left, right, first, count, into):
    rows, ff_local = left.shape
    model_dim = right.shape[1]
    tile = outer_tile(ff_local)
    depth = min(4, count)
    operands = [left, right] + ([] if into is None else [into])
    return pl.pallas_call(
        functools.partial(outer_kernel, tile, first, count),
        out_shape=jax.ShapeDtypeStruct((ff_local, model_dim), F32),
        in_specs=[VMEM_SPEC, VMEM_SPEC, ANY_SPEC][: len(operands)],
        out_specs=ANY_SPEC,
        input_output_aliases={} if into is None else {2: 0},
        scratch_shapes=[
            pltpu.VMEM((depth, tile, model_dim), F32),
            pltpu.SemaphoreType.DMA((depth,)),
        ],
        compiler_params=pltpu.CompilerParams(vmem_limit_bytes=16 * 1024 * 1024),
        cost_estimate=pl.CostEstimate(
            flops=2 * rows * count * tile * model_dim,
            bytes_accessed=4 * count * tile * model_dim,
            transcendentals=0,
        ),
    )(*operands)


class Outers:
    def __init__(self, factors, windows):
        tiles = factors[0][0].shape[1] // outer_tile(factors[0][0].shape[1])
        self.factors = factors
        self.results = [None] * len(factors)
        total = tiles * len(factors)
        shares = SHARES if windows == len(SHARES) else (1,) * windows
        ends = [total * sum(shares[: i + 1]) // sum(shares) for i in range(windows)]
        self.pieces = []
        for begin, end in zip([0] + ends[:-1], ends):
            piece = []
            while begin < end:
                which, first = divmod(begin, tiles)
                count = min(end - begin, tiles - first)
                piece.append((which, first, count))
                begin += count
            self.pieces.append(piece)

    def beside(self, received, sent):
        for which, first, count in self.pieces.pop(0):
            left, right = self.factors[which]
            left, _ = lax.optimization_barrier((left, sent))
            result = weight_grad(left, right, first, count, self.results[which])
            received, self.results[which] = lax.optimization_barrier((received, result))
        return received


def norm_backward(x, grad, row_sum, gain, weight):
    inverse = lax.rsqrt(jnp.mean(x * x, axis=1, keepdims=True) + EPSILON)
    hat = x * inverse
    router = jax.nn.sigmoid(jnp.sum(x * weight, axis=1, keepdims=True))
    hat_grad = grad * gain
    norm_part = inverse * (hat_grad - hat * jnp.mean(hat_grad * hat, axis=1, keepdims=True))
    return norm_part + row_sum * (1.0 - router) * weight


def delta_kernel(
    pay_ref, sum_ref, stat_ref, last_ref, gain_ref, router_ref, out_ref, gain_out_ref, router_out_ref
):
    middle = out_ref.shape[1]
    x = pay_ref[...].astype(F32)[:BLOCK, : 2 * middle]
    sums = sum_ref[...] + last_ref[0].astype(F32)
    far = last_ref[1].astype(F32)
    stats = stat_ref[...] + far[:BLOCK] + far[BLOCK:]
    grad = jnp.concatenate([sums[:BLOCK, :middle], sums[BLOCK:, :middle]], axis=1)
    row_sum = sums[:BLOCK, middle : middle + 1]
    delta = norm_backward(x, grad, row_sum, gain_ref[...], router_ref[...].astype(F32))
    out_ref[...] = jnp.concatenate([delta[:, :middle], delta[:, middle:]], axis=0).astype(BF16)
    for second in range(2):
        cols = slice(second * middle, (second + 1) * middle)
        gain_out_ref[:, cols] = stats[second : second + 1, :middle]
        router_out_ref[:, cols] = stats[2 + second : 3 + second, :middle]


def delta_rows(pay, sums, stats, last, gain, router):
    row = jax.ShapeDtypeStruct(gain.shape, F32)
    return pl.pallas_call(
        delta_kernel,
        out_shape=(jax.ShapeDtypeStruct((8, sums.shape[1] - LANES), BF16), row, row),
        in_specs=[VMEM_SPEC] * 6,
        out_specs=(VMEM_SPEC,) * 3,
        compiler_params=pltpu.CompilerParams(vmem_limit_bytes=SMALL_LIMIT),
    )(pay, sums, stats, last, gain, router)


def shared_kernel(x_ref, sum_ref, gain_ref, router_ref, out_ref):
    model_dim = x_ref.shape[1]
    delta = norm_backward(
        x_ref[...].astype(F32),
        sum_ref[:, :model_dim],
        sum_ref[:, model_dim : model_dim + 1],
        gain_ref[...],
        router_ref[...].astype(F32),
    )
    out_ref[...] = delta.astype(BF16)


def shared_rows(x, sums, gain, router):
    return pl.pallas_call(
        shared_kernel,
        out_shape=jax.ShapeDtypeStruct(x.shape, BF16),
        in_specs=[VMEM_SPEC] * 4,
        out_specs=VMEM_SPEC,
        compiler_params=pltpu.CompilerParams(
            vmem_limit_bytes=(4 if x.shape[0] <= 8 else 28) * 1024 * 1024
        ),
    )(x, sums, gain, router)


def add_kernel(
    here_ref, blocks_ref, dest_ref, other_blocks_ref, other_dest_ref,
    own_ref, back_ref, other_ref, other_back_ref, grad_ref, out_ref,
):
    middle = own_ref.shape[1]
    lower = here_ref[0] == 0
    mine = route_slots(blocks_ref, dest_ref, here_ref[1])
    theirs = route_slots(other_blocks_ref, other_dest_ref, here_ref[1])
    out_ref[...] = grad_ref[...]
    row = lax.broadcasted_iota(jnp.int32, (GROUP, 1), 0)

    def add(block, used, deltas):
        at = pl.ds(pl.multiple_of((block * BLOCK) // GROUP * GROUP, GROUP), GROUP)
        mask = (row // BLOCK == block % (GROUP // BLOCK)) & used
        for half in range(2):
            cols = slice(half * middle, (half + 1) * middle)
            four = deltas[half * BLOCK : (half + 1) * BLOCK, :]
            spread = jnp.concatenate([four] * (GROUP // BLOCK), axis=0)
            out_ref[at, cols] = (
                out_ref[at, cols].astype(F32) + jnp.where(mask, spread, 0.0)
            ).astype(BF16)

    for slot, (own, other) in enumerate(((own_ref, other_ref), (back_ref, other_back_ref))):
        block = jnp.where(lower, theirs[slot][0], mine[slot][0])
        used = jnp.where(lower, theirs[slot][1], mine[slot][1])
        deltas = jnp.where(lower, other[...].astype(F32), own[...].astype(F32))
        add(block, used, deltas)
    for slot, own in enumerate((own_ref, back_ref)):
        add(mine[slot][0], mine[slot][1] & lower, own[...].astype(F32))


def add_rows(here, routes, deltas, grad):
    return pl.pallas_call(
        add_kernel,
        out_shape=jax.ShapeDtypeStruct(grad.shape, BF16),
        in_specs=[SMEM_SPEC] * 5 + [VMEM_SPEC] * 5,
        out_specs=VMEM_SPEC,
        compiler_params=pltpu.CompilerParams(vmem_limit_bytes=SMALL_LIMIT),
    )(here, *routes, *deltas, grad)


def on_device(saved, grad_out, route_blocks, route_dest, gain, w_router, w_gate, w_up, w_down):
    sections = lax.axis_size("pipe")
    peers = lax.axis_size("ctx")
    here = jnp.stack([lax.axis_index("pipe"), lax.axis_index("ctx")]).astype(jnp.int32)
    tokens = saved[0]
    model_dim = tokens.shape[1]

    swap = [(i, sections - 1 - i) for i in range(sections)]
    routes = (
        route_blocks,
        route_dest,
        lax.ppermute(route_blocks, "pipe", swap),
        lax.ppermute(route_dest, "pipe", swap),
    )
    kept_rows, handed_rows = pick_blocks(here, routes, tokens, grad_out)
    pay_mine, pair, gate_w = first_pair(kept_rows, handed_rows, w_gate[0])
    pay, (up_w, down_w) = gather_all(pair, (w_up[0], w_down[0]))
    few = 2 * BLOCK
    run = functools.partial(layer_pass, here, pay, gain, w_router)
    state, saved_parts = run((gate_w, up_w, down_w), few)
    hidden, normed, active, up_slope, shared_part, shared_x, case = saved_parts

    def corrected(count):
        def branch(state):
            weights = (w_gate[0], w_up[0], w_down[0])
            small = count == few
            if small:
                part, x = shared_part, shared_x
            else:
                part, x = run(weights, count, stream=True)[1][4:6]
            sums, fetched = sum_all(part, weights if small else ())
            upper = shared_rows(x, sums, gain, w_router)
            upper = lax.ppermute(upper, "pipe", swap)
            again = (upper, active, up_slope, hidden)
            return run(fetched if small else weights, few, again, stream=not small)[0]

        return branch

    state = lax.switch(
        case[0], (lambda state: state, corrected(few), corrected(peers * BLOCK)), state
    )
    gate_grad, up_grad, scaled, keep, sent, stats = state

    outers = Outers(
        ((hidden, scaled), (gate_grad, normed), (up_grad, normed)), len(hop_order(peers)) + 2
    )
    keep = keep.reshape((peers // 2,) + keep.shape[2:])
    sums, stats, last = scatter_sum(keep, sent, stats, outers)
    delta, grad_gain, grad_router = delta_rows(pay_mine, sums, stats, last, gain, w_router)
    back = lax.ppermute(delta, "ctx", [(i, (i - 1) % peers) for i in range(peers)])
    other = lax.ppermute(delta, "pipe", swap)
    back = outers.beside(back, delta)
    other_back = outers.beside(lax.ppermute(back, "pipe", swap), back)
    grad_inputs = add_rows(here, routes, (delta, back, other, other_back), grad_out)
    grad_down, grad_gate, grad_up = outers.results
    return (
        grad_inputs[None],
        grad_gate[None],
        grad_up[None],
        grad_down[None],
        grad_gain,
        grad_router,
    )


def solution(mesh):
    split = P("pipe", "ctx", None)
    row = P("pipe", None)
    return jax.shard_map(
        on_device,
        mesh=mesh,
        in_specs=(split, P("ctx", None), split, split, row, row, split, split, split),
        out_specs=(split, split, split, split, row, row),
        check_vma=False,
    )
```

```python
import functools

import jax
import jax.numpy as jnp
from jax import lax
from jax.experimental import pallas as pl
from jax.experimental.pallas import tpu as pltpu
from jax.sharding import PartitionSpec as P

BLOCK = 4
EPSILON = 1e-05
LANES = 128
CHUNK = 512
WIDE = 1024
PLAN_TILES = 14
PLAN = (((0, 0, 14),), ((1, 0, 8),), ((2, 0, 11),), ((1, 8, 6), (2, 11, 3)))
GROUP = 16
TILE = 256
VMEM_LIMIT = 10 * 1024 * 1024
STREAM_LIMIT = 32 * 1024 * 1024
SMALL_LIMIT = 6 * 1024 * 1024

F32 = jnp.float32
BF16 = jnp.bfloat16
VMEM_SPEC = pl.BlockSpec(memory_space=pltpu.VMEM)
SMEM_SPEC = pl.BlockSpec(memory_space=pltpu.SMEM)
ANY_SPEC = pl.BlockSpec(memory_space=pl.ANY)
HBM_SPEC = pl.BlockSpec(memory_space=pltpu.HBM)


def hop_order(peers):
    masks = []
    step = 1
    while step < peers:
        masks.append(step)
        step *= 2
    return masks[2:] + masks[:2][::-1]


def exchange(block, mask):
    peers = lax.axis_size("ctx")
    return lax.ppermute(block, "ctx", [(i, i ^ mask) for i in range(peers)])


def choose_kernel(kept_ref, came_ref, far_kept_ref, far_came_ref, pair_ref):
    used = kept_ref.shape[1] - LANES + 3

    def choose(kept, came):
        keeps = kept[:, used : used + 1].astype(F32) > 0.5
        return jnp.where(keeps, kept[...].astype(F32), came[...].astype(F32)).astype(BF16)

    pair_ref[0] = choose(kept_ref, came_ref)
    pair_ref[1] = choose(far_kept_ref, far_came_ref)


def first_pair(kept, handed, weight):
    peers = lax.axis_size("ctx")
    mask = hop_order(peers)[0]
    came = lax.ppermute(handed, "ctx", [(i, (i + 1) % peers) for i in range(peers)])
    far_kept = exchange(kept, mask)
    far_came = lax.ppermute(handed, "ctx", [(i, ((i + 1) % peers) ^ mask) for i in range(peers)])
    came, weight = beside(came, handed, weight)
    pair = pl.pallas_call(
        choose_kernel,
        out_shape=jax.ShapeDtypeStruct((2,) + kept.shape, BF16),
        in_specs=[VMEM_SPEC] * 4,
        out_specs=VMEM_SPEC,
        compiler_params=pltpu.CompilerParams(vmem_limit_bytes=SMALL_LIMIT),
    )(kept, came, far_kept, far_came)
    return pair, weight


def gather_all(held, weights):
    masks = hop_order(lax.axis_size("ctx"))
    cut = (held.shape[2] - LANES) // 2
    up_w, down_w = weights
    for mask in masks[1:-2]:
        came = exchange(held, mask)
        if mask == masks[-3]:
            came, up_w = beside(came, held, up_w)
        held = jnp.concatenate([held, came], axis=0)
    near, far = masks[-2:]
    first, second = held[:, :, :cut], held[:, :, cut:]
    count = held.shape[0]
    first_near = exchange(first, near)
    second_far = exchange(second, far)
    second_far, down_w = beside(second_far, second, down_w)
    first = jnp.concatenate([first, first_near], axis=0)
    second_pair = jnp.concatenate([second, second_far], axis=0)
    first_far = exchange(first, far)
    second_near = exchange(second_pair, near)
    first = jnp.concatenate([first, first_far], axis=0)
    second = jnp.concatenate(
        [second, second_near[:count], second_far, second_near[count:]], axis=0
    )
    return (first, second), (up_w, down_w)


def scatter_sum(keep, sent, outers):
    peers = lax.axis_size("ctx")
    half = keep.shape[0] - 2
    chunks, stats = keep[:half], keep[half, :BLOCK]
    masks = hop_order(peers)[::-1]
    for step, mask in enumerate(masks):
        if step > 0:
            half = chunks.shape[0] // 2
            high = lax.reduce_precision(stats, 8, 7)
            both = jnp.concatenate([high, stats - high], axis=0).astype(BF16)
            sent = jnp.concatenate([chunks[half:].astype(BF16), both[None]], axis=0)
        received = exchange(sent, mask)
        if mask != masks[-1]:
            received = outers.beside(received, sent)
            chunks = chunks[:half] + received[:half].astype(F32)
            stats = stats + received[half, :BLOCK].astype(F32)
            stats = stats + received[half, BLOCK:].astype(F32)
    near = lax.ppermute(
        chunks[0].astype(BF16), "ctx", [(i, (i - 1) % peers) for i in range(peers)]
    )
    far = lax.ppermute(sent[0], "ctx", [(i, ((i ^ masks[-1]) - 1) % peers) for i in range(peers)])
    received = outers.beside(received, sent)
    return chunks[0], stats, received, near, far


def sum_all(rows, weights):
    total = rows.astype(F32)
    fetched = []
    for mask in hop_order(lax.axis_size("ctx")):
        sent = total.astype(BF16)
        received = exchange(sent, mask)
        if len(fetched) < len(weights):
            received, weight = beside(received, sent, weights[len(fetched)])
            fetched.append(weight)
        total = total + received.astype(F32)
    return total, fetched


def contract_last(left_side, right_side):
    return lax.dot_general(
        left_side, right_side, (((1,), (1,)), ((), ())), preferred_element_type=F32
    )


def route_slots(blocks_ref, dest_ref, me):
    first, second = blocks_ref[0, 0, 0], blocks_ref[0, 0, 1]
    kept = dest_ref[0, 0, 0] == me
    handed = jnp.where(kept, dest_ref[0, 0, 1], dest_ref[0, 0, 0]) >= 0
    return (first, kept), (jnp.where(kept, second, first), handed)


def pick_kernel(
    blocks_ref, dest_ref, other_blocks_ref, other_dest_ref, saved_ref, grad_ref,
    keep_ref, hand_ref, groups, sems,
):
    model_dim = saved_ref.shape[1]
    me = lax.axis_index("ctx")
    slots = route_slots(blocks_ref, dest_ref, me)
    copies = []
    for slot, (block, _) in enumerate(slots):
        first = pl.multiple_of((block * BLOCK) // GROUP * GROUP, GROUP)
        for kind, source in enumerate((saved_ref, grad_ref)):
            copy = pltpu.make_async_copy(
                source.at[pl.ds(first, GROUP)], groups.at[slot, kind], sems.at[slot, kind]
            )
            copy.start()
            copies.append(copy)
    for copy in copies:
        copy.wait()
    rows = lax.broadcasted_iota(jnp.int32, (8, GROUP), 0)
    cols = lax.broadcasted_iota(jnp.int32, (8, GROUP), 1)
    lane = lax.broadcasted_iota(jnp.int32, (8, LANES), 1)
    for slot, out in enumerate((keep_ref, hand_ref)):
        block, used = slots[slot]
        offset = (block * BLOCK) % GROUP
        from_saved = jnp.where((rows < BLOCK) & (cols == offset + rows), 1.0, 0.0).astype(BF16)
        from_grad = jnp.where(
            (rows >= BLOCK) & (cols == offset + rows - BLOCK), 1.0, 0.0
        ).astype(BF16)
        for start in range(0, model_dim, CHUNK):
            at = slice(start, start + CHUNK)
            picked = jnp.dot(
                from_saved, groups[slot, 0, :, at], preferred_element_type=F32
            ) + jnp.dot(from_grad, groups[slot, 1, :, at], preferred_element_type=F32)
            out[:, at] = picked.astype(BF16)
        shared = jnp.int32(0)
        for j in range(2):
            same = (other_blocks_ref[0, 0, j] == block) & (other_dest_ref[0, 0, j] >= 0)
            shared = jnp.where(same & used, 1, shared)
        meta = jnp.zeros((8, LANES), F32)
        for index, value in enumerate((me, block, shared, used.astype(jnp.int32))):
            meta = jnp.where(lane == index, value.astype(F32), meta)
        out[:, model_dim:] = meta.astype(BF16)


def pick_blocks(routes, saved, grad):
    model_dim = saved.shape[1]
    shape = jax.ShapeDtypeStruct((8, model_dim + LANES), BF16)
    return pl.pallas_call(
        pick_kernel,
        out_shape=(shape, shape),
        in_specs=[SMEM_SPEC] * 4 + [ANY_SPEC, ANY_SPEC],
        out_specs=(VMEM_SPEC, VMEM_SPEC),
        scratch_shapes=[
            pltpu.VMEM((2, 2, GROUP, model_dim), BF16),
            pltpu.SemaphoreType.DMA((2, 2)),
        ],
        compiler_params=pltpu.CompilerParams(vmem_limit_bytes=SMALL_LIMIT),
    )(
        *(pltpu.with_memory_space_constraint(a, pltpu.HBM) for a in routes[:2]),
        *routes[2:],
        *(pltpu.with_memory_space_constraint(a, pltpu.HBM) for a in (saved, grad)),
    )


def layer_kernel(with_delta, stream, tile, *refs):
    if with_delta:
        delta_ref, active_ref, up_slope_ref, hidden_ref = refs[:4]
        refs = refs[4:]
    first_ref, second_ref, gain_ref, router_ref, gate_w, up_w, down_w = refs[:7]
    refs = refs[7:]
    gate_grad_ref, up_grad_ref, scaled_ref, keep_ref, sent_ref = refs[:5]
    refs = refs[5:]
    if not with_delta:
        hidden_ref, normed_ref, active_ref, up_slope_ref = refs[:4]
        shared_part_ref, shared_x_ref, case_ref = refs[4:7]
        refs = refs[7:]
    picked_s, up_s, gate_rows, up_rows = refs[:4]
    waits = ()
    if stream:
        *held, sems = refs[4:]
        copies = [
            pltpu.make_async_copy(source, target, sems.at[index])
            for index, (source, target) in enumerate(zip((down_w, gate_w, up_w), held))
        ]
        for copy in copies:
            copy.start()
        down_w, gate_w, up_w = held
        waits = (copies[:1], copies[1:]) if with_delta else (copies, ())
    half_pairs = first_ref.shape[0]
    quarter = half_pairs // 2
    rows = half_pairs * 8
    model_dim = scaled_ref.shape[1]
    ff_local = gate_grad_ref.shape[0]
    middle = model_dim // 2

    def split(ref, start, width):
        even = ref[:, 0, :, pl.ds(start, width)].astype(F32)
        odd = ref[:, 1, :, pl.ds(start, width)].astype(F32)
        low = lax.broadcasted_iota(jnp.int32, even.shape, 1) < BLOCK
        first = jnp.where(low, even, pltpu.roll(odd, BLOCK, 1)).reshape(rows, width)
        second = jnp.where(low, pltpu.roll(even, BLOCK, 1), odd).reshape(rows, width)
        return first, second

    def gather_chunk(c, carry):
        squares, logits = carry
        inner = pl.multiple_of(c * WIDE, WIDE)
        for ref, base in ((first_ref, 0), (second_ref, middle)):
            at = pl.ds(pl.multiple_of(inner + base, WIDE), WIDE)
            x, g = split(ref, inner, WIDE)
            picked_s[:, at] = x.astype(BF16)
            up_s[:, at] = g.astype(BF16)
            squares = squares + jnp.sum(x * x, axis=1, keepdims=True)
            logits = logits + jnp.sum(x * router_ref[:, at].astype(F32), axis=1, keepdims=True)
        return squares, logits

    zero = jnp.zeros((rows, 1), F32)
    squares, logits = lax.fori_loop(0, middle // WIDE, gather_chunk, (zero, zero))
    inverse = lax.rsqrt(squares * (1.0 / model_dim) + EPSILON)
    router = jax.nn.sigmoid(logits)

    meta, _ = split(second_ref, middle, LANES)
    lane = lax.broadcasted_iota(jnp.int32, (8, LANES), 1)
    pick = lax.broadcasted_iota(jnp.int32, (8, LANES), 0) == lane
    across = contract_last(jnp.where(pick, 1.0, 0.0).astype(BF16), meta.astype(BF16))
    key_row = across[0:1] * LANES + across[1:2]
    key_col = meta[:, 0:1] * LANES + meta[:, 1:2]
    row_a = lax.broadcasted_iota(jnp.int32, (rows, rows), 0)
    row_b = lax.broadcasted_iota(jnp.int32, (rows, rows), 1)
    ahead = (key_col < key_row) & (meta[:, 2:3] > 0.5) & (row_a % BLOCK == 0)
    rank = jnp.sum(jnp.where(ahead, 1.0, 0.0), axis=0, keepdims=True)
    place = rank.astype(jnp.int32) * BLOCK + row_b % BLOCK
    chosen = jnp.where((place == row_a) & (across[2:3] > 0.5), 1.0, 0.0).astype(BF16)
    if with_delta:
        lower = jnp.where(lax.axis_index("pipe") == 0, 1.0, 0.0).astype(BF16)
        spread = chosen[: delta_ref.shape[0]] * lower
    else:
        blocks = jnp.sum(across[2:3]) * (1.0 / BLOCK)
        few = shared_x_ref.shape[0] // BLOCK
        case_ref[0] = jnp.where(blocks > few + 0.5, 2, jnp.where(blocks > 0.5, 1, 0))
        chosen = chosen[: shared_x_ref.shape[0]]

    def scale_chunk(c, carry):
        at = pl.ds(pl.multiple_of(c * WIDE, WIDE), WIDE)
        x = picked_s[:, at]
        upstream = up_s[:, at].astype(F32)
        if with_delta:
            added = lax.dot_general(
                spread, delta_ref[:, at], (((0,), (0,)), ((), ())), preferred_element_type=F32
            )
            upstream = (upstream + added).astype(BF16).astype(F32)
        else:
            normed_ref[:, at] = (x.astype(F32) * inverse * gain_ref[:, at]).astype(BF16)
            shared_x_ref[:, at] = jnp.dot(chosen, x, preferred_element_type=F32).astype(BF16)
        scaled_ref[:, at] = (router * upstream).astype(BF16)
        return carry

    lax.fori_loop(0, model_dim // WIDE, scale_chunk, 0)

    row_sums = zero
    for copy in waits[0] if stream else ():
        copy.wait()
    for begin in range(0, ff_local, tile):
        at = slice(begin, min(begin + tile, ff_local))
        hidden_grad = contract_last(down_w[at, :], scaled_ref[...])
        if with_delta:
            activated = active_ref[at, :]
            up_slope = up_slope_ref[at, :]
        else:
            gate = contract_last(gate_w[at, :], normed_ref[...])
            up = contract_last(up_w[at, :], normed_ref[...])
            sigma = jax.nn.sigmoid(gate)
            activated = gate * sigma
            up_slope = up * (sigma * (1.0 + gate * (1.0 - sigma)))
            hidden = (activated * up).astype(BF16)
            hidden_ref[at, :] = hidden
            active_ref[at, :] = activated
            up_slope_ref[at, :] = up_slope
        gate_grad = (hidden_grad * up_slope).astype(BF16)
        up_grad = (hidden_grad * activated).astype(BF16)
        gate_grad_ref[at, :] = gate_grad
        up_grad_ref[at, :] = up_grad
        gate_rows[:, at] = gate_grad.T
        up_rows[:, at] = up_grad.T
        if with_delta:
            hidden = hidden_ref[at, :]
        row_sums = row_sums + jnp.sum(hidden_grad * hidden.astype(F32), axis=0, keepdims=True).T
    logit_part = row_sums * (1.0 - router)

    low = lax.broadcasted_iota(jnp.int32, (half_pairs, 8, 1), 1) < BLOCK

    def store(even, odd, at):
        keep_ref[:quarter, 0, :, at] = even[:quarter]
        keep_ref[:quarter, 1, :, at] = odd[:quarter]
        for q in range(quarter):
            sent_ref[2 * q, :, at] = even[quarter + q].astype(BF16)
            sent_ref[2 * q + 1, :, at] = odd[quarter + q].astype(BF16)

    for copy in waits[1] if stream else ():
        copy.wait()

    def out_chunk(c, carry):
        at = pl.ds(pl.multiple_of(c * WIDE, WIDE), WIDE)
        halves = []
        gains = []
        routers = []
        for second in range(2):
            cols = pl.ds(pl.multiple_of(c * WIDE + second * middle, WIDE), WIDE)
            grad = jnp.dot(
                gate_rows[...], gate_w[:, cols], preferred_element_type=F32
            ) + jnp.dot(up_rows[...], up_w[:, cols], preferred_element_type=F32)
            x = picked_s[:, cols].astype(F32)
            gains.append(jnp.sum(grad * (x * inverse), axis=0, keepdims=True))
            routers.append(jnp.sum(logit_part * x, axis=0, keepdims=True))
            if not with_delta:
                shared_part_ref[:, cols] = jnp.dot(
                    chosen, grad.astype(BF16), preferred_element_type=F32
                ).astype(BF16)
            halves.append(grad.reshape(half_pairs, 8, WIDE))
        a, b = halves
        store(
            jnp.where(low, a, pltpu.roll(b, BLOCK, 1)),
            jnp.where(low, pltpu.roll(a, BLOCK, 1), b),
            at,
        )
        stats = jnp.concatenate(gains + routers, axis=0)
        high = stats.astype(BF16).astype(F32)
        keep_ref[quarter, 0, :BLOCK, at] = stats
        sent_ref[2 * quarter, :, at] = jnp.concatenate([high, stats - high], axis=0).astype(BF16)
        return carry

    lax.fori_loop(0, middle // WIDE, out_chunk, 0)
    wide = jnp.broadcast_to(row_sums, (rows, LANES))
    if not with_delta:
        shared_part_ref[:, model_dim:] = jnp.dot(
            chosen, wide.astype(BF16), preferred_element_type=F32
        ).astype(BF16)
    wide = wide.reshape(half_pairs, 8, LANES)
    store(wide, pltpu.roll(wide, BLOCK, 1), pl.ds(middle, LANES))
    keep_ref[quarter, 0, :BLOCK, middle:] = jnp.zeros((BLOCK, LANES), F32)
    sent_ref[2 * quarter, :, middle:] = jnp.zeros((8, LANES), BF16)


def fetch_kernel(source_ref, out_ref, sems):
    parts = sems.shape[0]
    size = source_ref.shape[0] // parts
    copies = []
    for part in range(parts):
        at = pl.ds(part * size, size)
        copy = pltpu.make_async_copy(source_ref.at[at], out_ref.at[at], sems.at[part])
        copy.start()
        copies.append(copy)
    for copy in copies:
        copy.wait()


def fetch(weight):
    return pl.pallas_call(
        fetch_kernel,
        out_shape=pltpu.VMEM(weight.shape, weight.dtype),
        in_specs=[HBM_SPEC],
        out_specs=VMEM_SPEC,
        scratch_shapes=[pltpu.SemaphoreType.DMA((7,))],
        compiler_params=pltpu.CompilerParams(vmem_limit_bytes=8 * 1024 * 1024),
        cost_estimate=pl.CostEstimate(
            flops=0, bytes_accessed=2 * weight.size, transcendentals=0
        ),
    )(pltpu.with_memory_space_constraint(weight, pltpu.HBM))


def beside(received, sent, weight):
    weight, _ = lax.optimization_barrier((weight, sent))
    fetched = fetch(weight)
    received, fetched = lax.optimization_barrier((received, fetched))
    return received, fetched


def layer_pass(pay, gain, router, weights, few, again=None, stream=False):
    peers = pay[0].shape[0]
    rows = peers * BLOCK
    ff_local, model_dim = weights[0].shape
    wide = model_dim // 2 + LANES
    pairs = [part.reshape((peers // 2, 2) + part.shape[1:]) for part in pay]
    if not stream:
        weights = [pltpu.with_memory_space_constraint(w, pltpu.VMEM) for w in weights]
    operands = [*pairs, gain, router, *weights]
    in_specs = [VMEM_SPEC] * 4 + [ANY_SPEC if stream else VMEM_SPEC] * 3
    scratch = [pltpu.VMEM((rows, model_dim), BF16)] * 2 + [pltpu.VMEM((rows, ff_local), BF16)] * 2
    if stream:
        scratch += [pltpu.VMEM((ff_local, model_dim), BF16)] * 3
        scratch += [pltpu.SemaphoreType.DMA((3,))]
    small = jax.ShapeDtypeStruct((ff_local, rows), BF16)
    large = jax.ShapeDtypeStruct((rows, model_dim), BF16)
    tall = jax.ShapeDtypeStruct((ff_local, rows), F32)
    out_shape = [
        small,
        small,
        large,
        jax.ShapeDtypeStruct((peers // 4 + 1, 2, 8, wide), F32),
        jax.ShapeDtypeStruct((peers // 2 + 1, 8, wide), BF16),
    ]
    out_specs = [VMEM_SPEC] * len(out_shape)
    if again is None:
        out_shape += [
            small,
            large,
            tall,
            tall,
            jax.ShapeDtypeStruct((few, model_dim + LANES), BF16),
            jax.ShapeDtypeStruct((few, model_dim), BF16),
            jax.ShapeDtypeStruct((1,), jnp.int32),
        ]
        out_specs += [VMEM_SPEC] * 6 + [SMEM_SPEC]
    else:
        operands = [*again, *operands]
        in_specs = [VMEM_SPEC] * len(again) + in_specs
    outs = pl.pallas_call(
        functools.partial(layer_kernel, again is not None, stream, TILE),
        out_shape=out_shape,
        in_specs=in_specs,
        out_specs=out_specs,
        scratch_shapes=scratch,
        compiler_params=pltpu.CompilerParams(
            vmem_limit_bytes=STREAM_LIMIT if stream else VMEM_LIMIT * max(1, rows // 64)
        ),
        cost_estimate=pl.CostEstimate(
            flops=10 * rows * ff_local * model_dim,
            bytes_accessed=6 * ff_local * model_dim,
            transcendentals=rows * ff_local,
        ),
    )(*operands)
    return tuple(outs[:5]), tuple(outs[5:])


def outer_kernel(tile, pieces, operands, *refs):
    outs = refs[operands : operands + len(pieces)]
    ring, sems = refs[-2:]
    depth = ring.shape[0]
    copies = []
    for (first, count, left, right), out_ref in zip(pieces, outs):
        for t in range(first, first + count):
            slot = len(copies) % depth
            if len(copies) >= depth:
                copies[len(copies) - depth].wait()
            at = pl.ds(t * tile, tile)
            ring[slot] = jnp.dot(refs[left][at, :], refs[right][...], preferred_element_type=F32)
            copy = pltpu.make_async_copy(ring.at[slot], out_ref.at[at], sems.at[slot])
            copy.start()
            copies.append(copy)
    for copy in copies[-depth:]:
        copy.wait()


def outer_tile(ff_local):
    return 64 if ff_local % 64 == 0 else 32


def weight_grads(pieces, factors, results):
    ff_local, rows = factors[0][0].shape
    model_dim = factors[0][1].shape[1]
    tile = outer_tile(ff_local)
    total = sum(count for _, _, count in pieces)
    depth = min(8, total)
    operands, specs, plan, aliases = [], [], [], {}

    def operand(value, spec):
        for index, known in enumerate(operands):
            if known is value:
                return index
        operands.append(value)
        specs.append(spec)
        return len(operands) - 1

    for index, (which, first, count) in enumerate(pieces):
        left, right = (operand(value, VMEM_SPEC) for value in factors[which])
        plan.append((first, count, left, right))
        if results[which] is not None:
            aliases[operand(results[which], ANY_SPEC)] = index
    return pl.pallas_call(
        functools.partial(outer_kernel, tile, tuple(plan), len(operands)),
        out_shape=(jax.ShapeDtypeStruct((ff_local, model_dim), F32),) * len(pieces),
        in_specs=specs,
        out_specs=(ANY_SPEC,) * len(pieces),
        input_output_aliases=aliases,
        scratch_shapes=[
            pltpu.VMEM((depth, tile, model_dim), F32),
            pltpu.SemaphoreType.DMA((depth,)),
        ],
        compiler_params=pltpu.CompilerParams(vmem_limit_bytes=16 * 1024 * 1024),
        cost_estimate=pl.CostEstimate(
            flops=2 * rows * total * tile * model_dim,
            bytes_accessed=4 * total * tile * model_dim,
            transcendentals=0,
        ),
    )(*operands)


class Outers:
    def __init__(self, factors, windows):
        tiles = factors[0][0].shape[0] // outer_tile(factors[0][0].shape[0])
        self.factors = factors
        self.results = [None] * len(factors)
        total = tiles * len(factors)
        if windows == len(PLAN) and tiles == PLAN_TILES:
            self.pieces = [list(piece) for piece in PLAN]
            return
        ends = [total * (i + 1) // windows for i in range(windows)]
        self.pieces = []
        for begin, end in zip([0] + ends[:-1], ends):
            piece = []
            while begin < end:
                which, first = divmod(begin, tiles)
                count = min(end - begin, tiles - first)
                piece.append((which, first, count))
                begin += count
            self.pieces.append(piece)

    def beside(self, received, sent):
        pieces = self.pieces.pop(0)
        if not pieces:
            return received
        factors = list(self.factors)
        which = pieces[0][0]
        left, right = factors[which]
        left, _ = lax.optimization_barrier((left, sent))
        factors[which] = (left, right)
        written = weight_grads(pieces, factors, self.results)
        received, *written = lax.optimization_barrier((received, *written))
        for (which, _, _), result in zip(pieces, written):
            self.results[which] = result
        return received


def norm_backward(x, grad, row_sum, gain, weight):
    inverse = lax.rsqrt(jnp.mean(x * x, axis=1, keepdims=True) + EPSILON)
    hat = x * inverse
    router = jax.nn.sigmoid(jnp.sum(x * weight, axis=1, keepdims=True))
    hat_grad = grad * gain
    norm_part = inverse * (hat_grad - hat * jnp.mean(hat_grad * hat, axis=1, keepdims=True))
    return norm_part + row_sum * (1.0 - router) * weight


def delta_kernel(
    kept_ref, handed_ref, sum_ref, stat_ref, last_ref, near_ref, far_ref, gain_ref, router_ref,
    out_ref, gain_out_ref, router_out_ref,
):
    middle = out_ref.shape[2]
    kept_sum = sum_ref[...] + last_ref[0].astype(F32)
    handed_sum = near_ref[...].astype(F32) + far_ref[...].astype(F32)
    for slot, (pay, sums) in enumerate(((kept_ref, kept_sum), (handed_ref, handed_sum))):
        x = pay[...].astype(F32)[:BLOCK, : 2 * middle]
        grad = jnp.concatenate([sums[:BLOCK, :middle], sums[BLOCK:, :middle]], axis=1)
        row_sum = sums[:BLOCK, middle : middle + 1]
        delta = norm_backward(x, grad, row_sum, gain_ref[...], router_ref[...].astype(F32))
        out_ref[slot] = jnp.concatenate([delta[:, :middle], delta[:, middle:]], axis=0).astype(
            BF16
        )
    more = last_ref[1].astype(F32)
    stats = stat_ref[...] + more[:BLOCK] + more[BLOCK:]
    for second in range(2):
        cols = slice(second * middle, (second + 1) * middle)
        gain_out_ref[:, cols] = stats[second : second + 1, :middle]
        router_out_ref[:, cols] = stats[2 + second : 3 + second, :middle]


def delta_rows(kept, handed, sums, gain, router):
    row = jax.ShapeDtypeStruct(gain.shape, F32)
    return pl.pallas_call(
        delta_kernel,
        out_shape=(jax.ShapeDtypeStruct((2, 8, sums[0].shape[1] - LANES), BF16), row, row),
        in_specs=[VMEM_SPEC] * 9,
        out_specs=(VMEM_SPEC,) * 3,
        compiler_params=pltpu.CompilerParams(vmem_limit_bytes=SMALL_LIMIT),
    )(kept, handed, *sums, gain, router)


def shared_kernel(x_ref, sum_ref, gain_ref, router_ref, out_ref):
    model_dim = x_ref.shape[1]
    delta = norm_backward(
        x_ref[...].astype(F32),
        sum_ref[:, :model_dim],
        sum_ref[:, model_dim : model_dim + 1],
        gain_ref[...],
        router_ref[...].astype(F32),
    )
    out_ref[...] = delta.astype(BF16)


def shared_rows(x, sums, gain, router):
    return pl.pallas_call(
        shared_kernel,
        out_shape=jax.ShapeDtypeStruct(x.shape, BF16),
        in_specs=[VMEM_SPEC] * 4,
        out_specs=VMEM_SPEC,
        compiler_params=pltpu.CompilerParams(
            vmem_limit_bytes=(4 if x.shape[0] <= 8 else 28) * 1024 * 1024
        ),
    )(x, sums, gain, router)


def add_kernel(
    blocks_ref, dest_ref, other_blocks_ref, other_dest_ref,
    own_ref, other_ref, grad_ref, out_ref,
):
    middle = own_ref.shape[2]
    lower = lax.axis_index("pipe") == 0
    me = lax.axis_index("ctx")
    mine = route_slots(blocks_ref, dest_ref, me)
    theirs = route_slots(other_blocks_ref, other_dest_ref, me)
    out_ref[...] = grad_ref[...]
    row = lax.broadcasted_iota(jnp.int32, (GROUP, 1), 0)

    def add(block, used, deltas):
        at = pl.ds(pl.multiple_of((block * BLOCK) // GROUP * GROUP, GROUP), GROUP)
        mask = (row // BLOCK == block % (GROUP // BLOCK)) & used
        for half in range(2):
            cols = slice(half * middle, (half + 1) * middle)
            four = deltas[half * BLOCK : (half + 1) * BLOCK, :]
            spread = jnp.concatenate([four] * (GROUP // BLOCK), axis=0)
            out_ref[at, cols] = (
                out_ref[at, cols].astype(F32) + jnp.where(mask, spread, 0.0)
            ).astype(BF16)

    for slot in range(2):
        block = jnp.where(lower, theirs[slot][0], mine[slot][0])
        used = jnp.where(lower, theirs[slot][1], mine[slot][1])
        add(block, used, jnp.where(lower, other_ref[slot].astype(F32), own_ref[slot].astype(F32)))
    for slot in range(2):
        add(mine[slot][0], mine[slot][1] & lower, own_ref[slot].astype(F32))


def add_rows(routes, own, other, grad):
    return pl.pallas_call(
        add_kernel,
        out_shape=jax.ShapeDtypeStruct(grad.shape, BF16),
        in_specs=[SMEM_SPEC] * 4 + [VMEM_SPEC] * 3,
        out_specs=VMEM_SPEC,
        compiler_params=pltpu.CompilerParams(vmem_limit_bytes=SMALL_LIMIT),
    )(*routes, own, other, grad)


def on_device(saved, grad_out, route_blocks, route_dest, gain, w_router, w_gate, w_up, w_down):
    sections = lax.axis_size("pipe")
    peers = lax.axis_size("ctx")
    tokens = saved[0]
    model_dim = tokens.shape[1]

    swap = [(i, sections - 1 - i) for i in range(sections)]
    routes = (
        route_blocks,
        route_dest,
        lax.ppermute(route_blocks, "pipe", swap),
        lax.ppermute(route_dest, "pipe", swap),
    )
    kept_rows, handed_rows = pick_blocks(routes, tokens, grad_out)
    pair, gate_w = first_pair(kept_rows, handed_rows, w_gate[0])
    pay, (up_w, down_w) = gather_all(pair, (w_up[0], w_down[0]))
    few = 2 * BLOCK
    run = functools.partial(layer_pass, pay, gain, w_router)
    state, saved_parts = run((gate_w, up_w, down_w), few)
    hidden, normed, active, up_slope, shared_part, shared_x, case = saved_parts

    def corrected(count):
        def branch(state):
            weights = (w_gate[0], w_up[0], w_down[0])
            small = count == few
            if small:
                part, x = shared_part, shared_x
            else:
                part, x = run(weights, count, stream=True)[1][4:6]
            sums, fetched = sum_all(part, weights if small else ())
            upper = shared_rows(x, sums, gain, w_router)
            upper = lax.ppermute(upper, "pipe", swap)
            again = (upper, active, up_slope, hidden)
            return run(fetched if small else weights, few, again, stream=not small)[0]

        return branch

    state = lax.switch(
        case[0], (lambda state: state, corrected(few), corrected(peers * BLOCK)), state
    )
    gate_grad, up_grad, scaled, keep, sent = state

    outers = Outers(((hidden, scaled), (gate_grad, normed), (up_grad, normed)), len(hop_order(peers)))
    sums = scatter_sum(keep.reshape((-1,) + keep.shape[2:]), sent, outers)
    delta, grad_gain, grad_router = delta_rows(kept_rows, handed_rows, sums, gain, w_router)
    other = lax.ppermute(delta, "pipe", swap)
    grad_inputs = add_rows(routes, delta, other, grad_out)
    grad_down, grad_gate, grad_up = outers.results
    return (
        grad_inputs[None],
        grad_gate[None],
        grad_up[None],
        grad_down[None],
        grad_gain,
        grad_router,
    )


def solution(mesh):
    split = P("pipe", "ctx", None)
    row = P("pipe", None)
    return jax.shard_map(
        on_device,
        mesh=mesh,
        in_specs=(split, P("ctx", None), split, split, row, row, split, split, split),
        out_specs=(split, split, split, split, row, row),
        check_vma=False,
    )
```

```python
import functools

import jax
import jax.numpy as jnp
from jax import lax
from jax.experimental import pallas as pl
from jax.experimental.pallas import tpu as pltpu
from jax.sharding import PartitionSpec as P

BLOCK = 4
EPSILON = 1e-05
LANES = 128
CHUNK = 512
WIDE = 1024
PLAN_TILES = 14
PLAN = (((0, 0, 14),), ((1, 0, 8),), ((2, 0, 11),), ((1, 8, 6), (2, 11, 3)))
GROUP = 16
TILE = 256
VMEM_LIMIT = 10 * 1024 * 1024
STREAM_LIMIT = 32 * 1024 * 1024
SMALL_LIMIT = 6 * 1024 * 1024

F32 = jnp.float32
BF16 = jnp.bfloat16
VMEM_SPEC = pl.BlockSpec(memory_space=pltpu.VMEM)
SMEM_SPEC = pl.BlockSpec(memory_space=pltpu.SMEM)
ANY_SPEC = pl.BlockSpec(memory_space=pl.ANY)
HBM_SPEC = pl.BlockSpec(memory_space=pltpu.HBM)


def hop_order(peers):
    masks = []
    step = 1
    while step < peers:
        masks.append(step)
        step *= 2
    return masks[2:] + masks[:2][::-1]


def exchange(block, mask):
    peers = lax.axis_size("ctx")
    return lax.ppermute(block, "ctx", [(i, i ^ mask) for i in range(peers)])


def choose_kernel(kept_ref, came_ref, far_kept_ref, far_came_ref, pair_ref):
    used = kept_ref.shape[1] - LANES + 3

    def choose(kept, came):
        keeps = kept[:, used : used + 1].astype(F32) > 0.5
        return jnp.where(keeps, kept[...].astype(F32), came[...].astype(F32)).astype(BF16)

    pair_ref[0] = choose(kept_ref, came_ref)
    pair_ref[1] = choose(far_kept_ref, far_came_ref)


def first_pair(kept, handed, weight):
    peers = lax.axis_size("ctx")
    mask = hop_order(peers)[0]
    came = lax.ppermute(handed, "ctx", [(i, (i + 1) % peers) for i in range(peers)])
    far_kept = exchange(kept, mask)
    far_came = lax.ppermute(handed, "ctx", [(i, ((i + 1) % peers) ^ mask) for i in range(peers)])
    came, weight = beside(came, handed, weight)
    pair = pl.pallas_call(
        choose_kernel,
        out_shape=jax.ShapeDtypeStruct((2,) + kept.shape, BF16),
        in_specs=[VMEM_SPEC] * 4,
        out_specs=VMEM_SPEC,
        compiler_params=pltpu.CompilerParams(vmem_limit_bytes=SMALL_LIMIT),
    )(kept, came, far_kept, far_came)
    return pair, weight


def gather_all(held, weights):
    masks = hop_order(lax.axis_size("ctx"))
    cut = (held.shape[2] - LANES) // 2
    up_w, down_w = weights
    for mask in masks[1:-2]:
        came = exchange(held, mask)
        if mask == masks[-3]:
            came, up_w = beside(came, held, up_w)
        held = jnp.concatenate([held, came], axis=0)
    near, far = masks[-2:]
    first, second = held[:, :, :cut], held[:, :, cut:]
    count = held.shape[0]
    first_near = exchange(first, near)
    second_far = exchange(second, far)
    second_far, down_w = beside(second_far, second, down_w)
    first = jnp.concatenate([first, first_near], axis=0)
    second_pair = jnp.concatenate([second, second_far], axis=0)
    first_far = exchange(first, far)
    second_near = exchange(second_pair, near)
    first = jnp.concatenate([first, first_far], axis=0)
    second = jnp.concatenate(
        [second, second_near[:count], second_far, second_near[count:]], axis=0
    )
    return (first, second), (up_w, down_w)


def scatter_sum(keep, sent, outers):
    peers = lax.axis_size("ctx")
    half = keep.shape[0] - 2
    chunks, stats = keep[:half], keep[half, :BLOCK]
    masks = hop_order(peers)[::-1]
    for step, mask in enumerate(masks):
        if step > 0:
            half = chunks.shape[0] // 2
            high = lax.reduce_precision(stats, 8, 7)
            both = jnp.concatenate([high, stats - high], axis=0).astype(BF16)
            sent = jnp.concatenate([chunks[half:].astype(BF16), both[None]], axis=0)
        received = exchange(sent, mask)
        if mask != masks[-1]:
            received = outers.beside(received, sent)
            chunks = chunks[:half] + received[:half].astype(F32)
            stats = stats + received[half, :BLOCK].astype(F32)
            stats = stats + received[half, BLOCK:].astype(F32)
    near = lax.ppermute(
        chunks[0].astype(BF16), "ctx", [(i, (i - 1) % peers) for i in range(peers)]
    )
    far = lax.ppermute(sent[0], "ctx", [(i, ((i ^ masks[-1]) - 1) % peers) for i in range(peers)])
    received = outers.beside(received, sent)
    return chunks[0], stats, received, near, far


def sum_all(rows, weights):
    total = rows.astype(F32)
    fetched = []
    for mask in hop_order(lax.axis_size("ctx")):
        sent = total.astype(BF16)
        received = exchange(sent, mask)
        if len(fetched) < len(weights):
            received, weight = beside(received, sent, weights[len(fetched)])
            fetched.append(weight)
        total = total + received.astype(F32)
    return total, fetched


def contract_last(left_side, right_side):
    return lax.dot_general(
        left_side, right_side, (((1,), (1,)), ((), ())), preferred_element_type=F32
    )


def route_slots(blocks_ref, dest_ref, me):
    first, second = blocks_ref[0, 0, 0], blocks_ref[0, 0, 1]
    kept = dest_ref[0, 0, 0] == me
    handed = jnp.where(kept, dest_ref[0, 0, 1], dest_ref[0, 0, 0]) >= 0
    return (first, kept), (jnp.where(kept, second, first), handed)


def pick_kernel(
    blocks_ref, dest_ref, other_blocks_ref, other_dest_ref, saved_ref, grad_ref,
    keep_ref, hand_ref, groups, sems,
):
    model_dim = saved_ref.shape[1]
    me = lax.axis_index("ctx")
    slots = route_slots(blocks_ref, dest_ref, me)
    copies = []
    for slot, (block, _) in enumerate(slots):
        first = pl.multiple_of((block * BLOCK) // GROUP * GROUP, GROUP)
        for kind, source in enumerate((saved_ref, grad_ref)):
            copy = pltpu.make_async_copy(
                source.at[pl.ds(first, GROUP)], groups.at[slot, kind], sems.at[slot, kind]
            )
            copy.start()
            copies.append(copy)
    for copy in copies:
        copy.wait()
    rows = lax.broadcasted_iota(jnp.int32, (8, GROUP), 0)
    cols = lax.broadcasted_iota(jnp.int32, (8, GROUP), 1)
    lane = lax.broadcasted_iota(jnp.int32, (8, LANES), 1)
    for slot, out in enumerate((keep_ref, hand_ref)):
        block, used = slots[slot]
        offset = (block * BLOCK) % GROUP
        from_saved = jnp.where((rows < BLOCK) & (cols == offset + rows), 1.0, 0.0).astype(BF16)
        from_grad = jnp.where(
            (rows >= BLOCK) & (cols == offset + rows - BLOCK), 1.0, 0.0
        ).astype(BF16)
        for start in range(0, model_dim, CHUNK):
            at = slice(start, start + CHUNK)
            picked = jnp.dot(
                from_saved, groups[slot, 0, :, at], preferred_element_type=F32
            ) + jnp.dot(from_grad, groups[slot, 1, :, at], preferred_element_type=F32)
            out[:, at] = picked.astype(BF16)
        shared = jnp.int32(0)
        for j in range(2):
            same = (other_blocks_ref[0, 0, j] == block) & (other_dest_ref[0, 0, j] >= 0)
            shared = jnp.where(same & used, 1, shared)
        meta = jnp.zeros((8, LANES), F32)
        for index, value in enumerate((me, block, shared, used.astype(jnp.int32))):
            meta = jnp.where(lane == index, value.astype(F32), meta)
        out[:, model_dim:] = meta.astype(BF16)


def pick_blocks(routes, saved, grad):
    model_dim = saved.shape[1]
    shape = jax.ShapeDtypeStruct((8, model_dim + LANES), BF16)
    return pl.pallas_call(
        pick_kernel,
        out_shape=(shape, shape),
        in_specs=[SMEM_SPEC] * 4 + [ANY_SPEC, ANY_SPEC],
        out_specs=(VMEM_SPEC, VMEM_SPEC),
        scratch_shapes=[
            pltpu.VMEM((2, 2, GROUP, model_dim), BF16),
            pltpu.SemaphoreType.DMA((2, 2)),
        ],
        compiler_params=pltpu.CompilerParams(vmem_limit_bytes=SMALL_LIMIT),
    )(
        *(pltpu.with_memory_space_constraint(a, pltpu.HBM) for a in routes[:2]),
        *routes[2:],
        *(pltpu.with_memory_space_constraint(a, pltpu.HBM) for a in (saved, grad)),
    )


def layer_kernel(with_delta, stream, tile, *refs):
    if with_delta:
        delta_ref, active_ref, up_slope_ref, hidden_ref = refs[:4]
        refs = refs[4:]
    first_ref, second_ref, gain_ref, router_ref, gate_w, up_w, down_w = refs[:7]
    refs = refs[7:]
    gate_grad_ref, up_grad_ref, scaled_ref, keep_ref, sent_ref = refs[:5]
    refs = refs[5:]
    if not with_delta:
        hidden_ref, normed_ref, active_ref, up_slope_ref = refs[:4]
        shared_part_ref, shared_x_ref, case_ref = refs[4:7]
        refs = refs[7:]
    picked_s, up_s, gate_rows, up_rows = refs[:4]
    waits = ()
    if stream:
        *held, sems = refs[4:]
        copies = [
            pltpu.make_async_copy(source, target, sems.at[index])
            for index, (source, target) in enumerate(zip((down_w, gate_w, up_w), held))
        ]
        for copy in copies:
            copy.start()
        down_w, gate_w, up_w = held
        waits = (copies[:1], copies[1:]) if with_delta else (copies, ())
    half_pairs = first_ref.shape[0]
    quarter = half_pairs // 2
    rows = half_pairs * 8
    model_dim = scaled_ref.shape[1]
    ff_local = gate_grad_ref.shape[0]
    middle = model_dim // 2

    def split(ref, start, width):
        even = ref[:, 0, :, pl.ds(start, width)].astype(F32)
        odd = ref[:, 1, :, pl.ds(start, width)].astype(F32)
        low = lax.broadcasted_iota(jnp.int32, even.shape, 1) < BLOCK
        first = jnp.where(low, even, pltpu.roll(odd, BLOCK, 1)).reshape(rows, width)
        second = jnp.where(low, pltpu.roll(even, BLOCK, 1), odd).reshape(rows, width)
        return first, second

    span = middle if rows <= 64 else WIDE

    def gather_chunk(c, carry):
        squares, logits = carry
        inner = pl.multiple_of(c * span, span)
        for ref, base in ((first_ref, 0), (second_ref, middle)):
            at = pl.ds(pl.multiple_of(inner + base, span), span)
            x, g = split(ref, inner, span)
            picked_s[:, at] = x.astype(BF16)
            up_s[:, at] = g.astype(BF16)
            squares = squares + jnp.sum(x * x, axis=1, keepdims=True)
            logits = logits + jnp.sum(x * router_ref[:, at].astype(F32), axis=1, keepdims=True)
        return squares, logits

    zero = jnp.zeros((rows, 1), F32)
    squares, logits = lax.fori_loop(0, middle // span, gather_chunk, (zero, zero))
    inverse = lax.rsqrt(squares * (1.0 / model_dim) + EPSILON)
    router = jax.nn.sigmoid(logits)

    meta, _ = split(second_ref, middle, LANES)
    lane = lax.broadcasted_iota(jnp.int32, (8, LANES), 1)
    pick = lax.broadcasted_iota(jnp.int32, (8, LANES), 0) == lane
    across = contract_last(jnp.where(pick, 1.0, 0.0).astype(BF16), meta.astype(BF16))
    key_row = across[0:1] * LANES + across[1:2]
    key_col = meta[:, 0:1] * LANES + meta[:, 1:2]
    row_a = lax.broadcasted_iota(jnp.int32, (rows, rows), 0)
    row_b = lax.broadcasted_iota(jnp.int32, (rows, rows), 1)
    ahead = (key_col < key_row) & (meta[:, 2:3] > 0.5) & (row_a % BLOCK == 0)
    rank = jnp.sum(jnp.where(ahead, 1.0, 0.0), axis=0, keepdims=True)
    place = rank.astype(jnp.int32) * BLOCK + row_b % BLOCK
    chosen = jnp.where((place == row_a) & (across[2:3] > 0.5), 1.0, 0.0).astype(BF16)
    if with_delta:
        lower = jnp.where(lax.axis_index("pipe") == 0, 1.0, 0.0).astype(BF16)
        spread = chosen[: delta_ref.shape[0]] * lower
    else:
        blocks = jnp.sum(across[2:3]) * (1.0 / BLOCK)
        few = shared_x_ref.shape[0] // BLOCK
        case_ref[0] = jnp.where(blocks > few + 0.5, 2, jnp.where(blocks > 0.5, 1, 0))
        chosen = chosen[: shared_x_ref.shape[0]]

    def scale_chunk(c, carry):
        at = pl.ds(pl.multiple_of(c * span, span), span)
        x = picked_s[:, at]
        upstream = up_s[:, at].astype(F32)
        if with_delta:
            added = lax.dot_general(
                spread, delta_ref[:, at], (((0,), (0,)), ((), ())), preferred_element_type=F32
            )
            upstream = (upstream + added).astype(BF16).astype(F32)
        else:
            normed_ref[:, at] = (x.astype(F32) * inverse * gain_ref[:, at]).astype(BF16)

            @pl.when(blocks > 0.5)
            def _():
                shared_x_ref[:, at] = jnp.dot(chosen, x, preferred_element_type=F32).astype(BF16)

        scaled_ref[:, at] = (router * upstream).astype(BF16)
        return carry

    lax.fori_loop(0, model_dim // span, scale_chunk, 0)

    row_sums = zero
    for copy in waits[0] if stream else ():
        copy.wait()
    for begin in range(0, ff_local, tile):
        at = slice(begin, min(begin + tile, ff_local))
        hidden_grad = contract_last(down_w[at, :], scaled_ref[...])
        if with_delta:
            activated = active_ref[at, :]
            up_slope = up_slope_ref[at, :]
        else:
            gate = contract_last(gate_w[at, :], normed_ref[...])
            up = contract_last(up_w[at, :], normed_ref[...])
            sigma = jax.nn.sigmoid(gate)
            activated = gate * sigma
            up_slope = up * (sigma * (1.0 + gate * (1.0 - sigma)))
            hidden = (activated * up).astype(BF16)
            hidden_ref[at, :] = hidden
            active_ref[at, :] = activated
            up_slope_ref[at, :] = up_slope
        gate_grad = (hidden_grad * up_slope).astype(BF16)
        up_grad = (hidden_grad * activated).astype(BF16)
        gate_grad_ref[at, :] = gate_grad
        up_grad_ref[at, :] = up_grad
        gate_rows[:, at] = gate_grad.T
        up_rows[:, at] = up_grad.T
        if with_delta:
            hidden = hidden_ref[at, :]
        row_sums = row_sums + jnp.sum(hidden_grad * hidden.astype(F32), axis=0, keepdims=True).T
    logit_part = row_sums * (1.0 - router)

    low = lax.broadcasted_iota(jnp.int32, (half_pairs, 8, 1), 1) < BLOCK

    def store(even, odd, at):
        keep_ref[:quarter, 0, :, at] = even[:quarter]
        keep_ref[:quarter, 1, :, at] = odd[:quarter]
        for q in range(quarter):
            sent_ref[2 * q, :, at] = even[quarter + q].astype(BF16)
            sent_ref[2 * q + 1, :, at] = odd[quarter + q].astype(BF16)

    for copy in waits[1] if stream else ():
        copy.wait()

    def out_chunk(c, carry):
        at = pl.ds(pl.multiple_of(c * WIDE, WIDE), WIDE)
        halves = []
        gains = []
        routers = []
        for second in range(2):
            cols = pl.ds(pl.multiple_of(c * WIDE + second * middle, WIDE), WIDE)
            grad = jnp.dot(
                gate_rows[...], gate_w[:, cols], preferred_element_type=F32
            ) + jnp.dot(up_rows[...], up_w[:, cols], preferred_element_type=F32)
            x = picked_s[:, cols].astype(F32)
            gains.append(jnp.sum(grad * (x * inverse), axis=0, keepdims=True))
            routers.append(jnp.sum(logit_part * x, axis=0, keepdims=True))
            if not with_delta:

                @pl.when(blocks > 0.5)
                def _(cols=cols, grad=grad):
                    shared_part_ref[:, cols] = jnp.dot(
                        chosen, grad.astype(BF16), preferred_element_type=F32
                    ).astype(BF16)

            halves.append(grad.reshape(half_pairs, 8, WIDE))
        a, b = halves
        store(
            jnp.where(low, a, pltpu.roll(b, BLOCK, 1)),
            jnp.where(low, pltpu.roll(a, BLOCK, 1), b),
            at,
        )
        stats = jnp.concatenate(gains + routers, axis=0)
        high = stats.astype(BF16).astype(F32)
        keep_ref[quarter, 0, :BLOCK, at] = stats
        sent_ref[2 * quarter, :, at] = jnp.concatenate([high, stats - high], axis=0).astype(BF16)
        return carry

    lax.fori_loop(0, middle // WIDE, out_chunk, 0)
    wide = jnp.broadcast_to(row_sums, (rows, LANES))
    if not with_delta:
        shared_part_ref[:, model_dim:] = jnp.dot(
            chosen, wide.astype(BF16), preferred_element_type=F32
        ).astype(BF16)
    wide = wide.reshape(half_pairs, 8, LANES)
    store(wide, pltpu.roll(wide, BLOCK, 1), pl.ds(middle, LANES))
    keep_ref[quarter, 0, :BLOCK, middle:] = jnp.zeros((BLOCK, LANES), F32)
    sent_ref[2 * quarter, :, middle:] = jnp.zeros((8, LANES), BF16)


def fetch_kernel(source_ref, out_ref, sems):
    parts = sems.shape[0]
    size = source_ref.shape[0] // parts
    copies = []
    for part in range(parts):
        at = pl.ds(part * size, size)
        copy = pltpu.make_async_copy(source_ref.at[at], out_ref.at[at], sems.at[part])
        copy.start()
        copies.append(copy)
    for copy in copies:
        copy.wait()


def fetch(weight):
    return pl.pallas_call(
        fetch_kernel,
        out_shape=pltpu.VMEM(weight.shape, weight.dtype),
        in_specs=[HBM_SPEC],
        out_specs=VMEM_SPEC,
        scratch_shapes=[pltpu.SemaphoreType.DMA((7,))],
        compiler_params=pltpu.CompilerParams(vmem_limit_bytes=8 * 1024 * 1024),
        cost_estimate=pl.CostEstimate(
            flops=0, bytes_accessed=2 * weight.size, transcendentals=0
        ),
    )(pltpu.with_memory_space_constraint(weight, pltpu.HBM))


def beside(received, sent, weight):
    weight, _ = lax.optimization_barrier((weight, sent))
    fetched = fetch(weight)
    received, fetched = lax.optimization_barrier((received, fetched))
    return received, fetched


def layer_pass(pay, gain, router, weights, few, again=None, stream=False):
    peers = pay[0].shape[0]
    rows = peers * BLOCK
    ff_local, model_dim = weights[0].shape
    wide = model_dim // 2 + LANES
    pairs = [part.reshape((peers // 2, 2) + part.shape[1:]) for part in pay]
    if not stream:
        weights = [pltpu.with_memory_space_constraint(w, pltpu.VMEM) for w in weights]
    operands = [*pairs, gain, router, *weights]
    in_specs = [VMEM_SPEC] * 4 + [ANY_SPEC if stream else VMEM_SPEC] * 3
    scratch = [pltpu.VMEM((rows, model_dim), BF16)] * 2 + [pltpu.VMEM((rows, ff_local), BF16)] * 2
    if stream:
        scratch += [pltpu.VMEM((ff_local, model_dim), BF16)] * 3
        scratch += [pltpu.SemaphoreType.DMA((3,))]
    small = jax.ShapeDtypeStruct((ff_local, rows), BF16)
    large = jax.ShapeDtypeStruct((rows, model_dim), BF16)
    tall = jax.ShapeDtypeStruct((ff_local, rows), F32)
    out_shape = [
        small,
        small,
        large,
        jax.ShapeDtypeStruct((peers // 4 + 1, 2, 8, wide), F32),
        jax.ShapeDtypeStruct((peers // 2 + 1, 8, wide), BF16),
    ]
    out_specs = [VMEM_SPEC] * len(out_shape)
    if again is None:
        out_shape += [
            small,
            large,
            tall,
            tall,
            jax.ShapeDtypeStruct((few, model_dim + LANES), BF16),
            jax.ShapeDtypeStruct((few, model_dim), BF16),
            jax.ShapeDtypeStruct((1,), jnp.int32),
        ]
        out_specs += [VMEM_SPEC] * 6 + [SMEM_SPEC]
    else:
        operands = [*again, *operands]
        in_specs = [VMEM_SPEC] * len(again) + in_specs
    outs = pl.pallas_call(
        functools.partial(layer_kernel, again is not None, stream, TILE),
        out_shape=out_shape,
        in_specs=in_specs,
        out_specs=out_specs,
        scratch_shapes=scratch,
        compiler_params=pltpu.CompilerParams(
            vmem_limit_bytes=STREAM_LIMIT if stream else VMEM_LIMIT * max(1, rows // 64)
        ),
        cost_estimate=pl.CostEstimate(
            flops=10 * rows * ff_local * model_dim,
            bytes_accessed=6 * ff_local * model_dim,
            transcendentals=rows * ff_local,
        ),
    )(*operands)
    return tuple(outs[:5]), tuple(outs[5:])


def outer_kernel(tile, pieces, operands, *refs):
    outs = refs[operands : operands + len(pieces)]
    ring, sems = refs[-2:]
    depth = ring.shape[0]
    copies = []
    for (first, count, left, right), out_ref in zip(pieces, outs):
        for t in range(first, first + count):
            slot = len(copies) % depth
            if len(copies) >= depth:
                copies[len(copies) - depth].wait()
            at = pl.ds(t * tile, tile)
            ring[slot] = jnp.dot(refs[left][at, :], refs[right][...], preferred_element_type=F32)
            copy = pltpu.make_async_copy(ring.at[slot], out_ref.at[at], sems.at[slot])
            copy.start()
            copies.append(copy)
    for copy in copies[-depth:]:
        copy.wait()


def outer_tile(ff_local):
    return 64 if ff_local % 64 == 0 else 32


def weight_grads(pieces, factors, results):
    ff_local, rows = factors[0][0].shape
    model_dim = factors[0][1].shape[1]
    tile = outer_tile(ff_local)
    total = sum(count for _, _, count in pieces)
    depth = min(8, total)
    operands, specs, plan, aliases = [], [], [], {}

    def operand(value, spec):
        for index, known in enumerate(operands):
            if known is value:
                return index
        operands.append(value)
        specs.append(spec)
        return len(operands) - 1

    for index, (which, first, count) in enumerate(pieces):
        left, right = (operand(value, VMEM_SPEC) for value in factors[which])
        plan.append((first, count, left, right))
        if results[which] is not None:
            aliases[operand(results[which], ANY_SPEC)] = index
    return pl.pallas_call(
        functools.partial(outer_kernel, tile, tuple(plan), len(operands)),
        out_shape=(jax.ShapeDtypeStruct((ff_local, model_dim), F32),) * len(pieces),
        in_specs=specs,
        out_specs=(ANY_SPEC,) * len(pieces),
        input_output_aliases=aliases,
        scratch_shapes=[
            pltpu.VMEM((depth, tile, model_dim), F32),
            pltpu.SemaphoreType.DMA((depth,)),
        ],
        compiler_params=pltpu.CompilerParams(vmem_limit_bytes=16 * 1024 * 1024),
        cost_estimate=pl.CostEstimate(
            flops=2 * rows * total * tile * model_dim,
            bytes_accessed=4 * total * tile * model_dim,
            transcendentals=0,
        ),
    )(*operands)


class Outers:
    def __init__(self, factors, windows):
        tiles = factors[0][0].shape[0] // outer_tile(factors[0][0].shape[0])
        self.factors = factors
        self.results = [None] * len(factors)
        total = tiles * len(factors)
        if windows == len(PLAN) and tiles == PLAN_TILES:
            self.pieces = [list(piece) for piece in PLAN]
            return
        ends = [total * (i + 1) // windows for i in range(windows)]
        self.pieces = []
        for begin, end in zip([0] + ends[:-1], ends):
            piece = []
            while begin < end:
                which, first = divmod(begin, tiles)
                count = min(end - begin, tiles - first)
                piece.append((which, first, count))
                begin += count
            self.pieces.append(piece)

    def beside(self, received, sent):
        pieces = self.pieces.pop(0)
        if not pieces:
            return received
        factors = list(self.factors)
        which = pieces[0][0]
        left, right = factors[which]
        left, _ = lax.optimization_barrier((left, sent))
        factors[which] = (left, right)
        written = weight_grads(pieces, factors, self.results)
        received, *written = lax.optimization_barrier((received, *written))
        for (which, _, _), result in zip(pieces, written):
            self.results[which] = result
        return received


def norm_backward(x, grad, row_sum, gain, weight):
    inverse = lax.rsqrt(jnp.mean(x * x, axis=1, keepdims=True) + EPSILON)
    hat = x * inverse
    router = jax.nn.sigmoid(jnp.sum(x * weight, axis=1, keepdims=True))
    hat_grad = grad * gain
    norm_part = inverse * (hat_grad - hat * jnp.mean(hat_grad * hat, axis=1, keepdims=True))
    return norm_part + row_sum * (1.0 - router) * weight


def delta_kernel(
    kept_ref, handed_ref, sum_ref, stat_ref, last_ref, near_ref, far_ref, gain_ref, router_ref,
    out_ref, gain_out_ref, router_out_ref,
):
    middle = out_ref.shape[2]
    kept_sum = sum_ref[...] + last_ref[0].astype(F32)
    handed_sum = near_ref[...].astype(F32) + far_ref[...].astype(F32)
    for slot, (pay, sums) in enumerate(((kept_ref, kept_sum), (handed_ref, handed_sum))):
        x = pay[...].astype(F32)[:BLOCK, : 2 * middle]
        grad = jnp.concatenate([sums[:BLOCK, :middle], sums[BLOCK:, :middle]], axis=1)
        row_sum = sums[:BLOCK, middle : middle + 1]
        delta = norm_backward(x, grad, row_sum, gain_ref[...], router_ref[...].astype(F32))
        out_ref[slot] = jnp.concatenate([delta[:, :middle], delta[:, middle:]], axis=0).astype(
            BF16
        )
    more = last_ref[1].astype(F32)
    stats = stat_ref[...] + more[:BLOCK] + more[BLOCK:]
    for second in range(2):
        cols = slice(second * middle, (second + 1) * middle)
        gain_out_ref[:, cols] = stats[second : second + 1, :middle]
        router_out_ref[:, cols] = stats[2 + second : 3 + second, :middle]


def delta_rows(kept, handed, sums, gain, router):
    row = jax.ShapeDtypeStruct(gain.shape, F32)
    return pl.pallas_call(
        delta_kernel,
        out_shape=(jax.ShapeDtypeStruct((2, 8, sums[0].shape[1] - LANES), BF16), row, row),
        in_specs=[VMEM_SPEC] * 9,
        out_specs=(VMEM_SPEC,) * 3,
        compiler_params=pltpu.CompilerParams(vmem_limit_bytes=SMALL_LIMIT),
    )(kept, handed, *sums, gain, router)


def shared_kernel(x_ref, sum_ref, gain_ref, router_ref, out_ref):
    model_dim = x_ref.shape[1]
    delta = norm_backward(
        x_ref[...].astype(F32),
        sum_ref[:, :model_dim],
        sum_ref[:, model_dim : model_dim + 1],
        gain_ref[...],
        router_ref[...].astype(F32),
    )
    out_ref[...] = delta.astype(BF16)


def shared_rows(x, sums, gain, router):
    return pl.pallas_call(
        shared_kernel,
        out_shape=jax.ShapeDtypeStruct(x.shape, BF16),
        in_specs=[VMEM_SPEC] * 4,
        out_specs=VMEM_SPEC,
        compiler_params=pltpu.CompilerParams(
            vmem_limit_bytes=(4 if x.shape[0] <= 8 else 28) * 1024 * 1024
        ),
    )(x, sums, gain, router)


def add_kernel(
    blocks_ref, dest_ref, other_blocks_ref, other_dest_ref,
    own_ref, other_ref, grad_ref, out_ref,
):
    middle = own_ref.shape[2]
    lower = lax.axis_index("pipe") == 0
    me = lax.axis_index("ctx")
    mine = route_slots(blocks_ref, dest_ref, me)
    theirs = route_slots(other_blocks_ref, other_dest_ref, me)
    out_ref[...] = grad_ref[...]
    row = lax.broadcasted_iota(jnp.int32, (GROUP, 1), 0)

    def add(block, used, deltas):
        at = pl.ds(pl.multiple_of((block * BLOCK) // GROUP * GROUP, GROUP), GROUP)
        mask = (row // BLOCK == block % (GROUP // BLOCK)) & used
        for half in range(2):
            cols = slice(half * middle, (half + 1) * middle)
            four = deltas[half * BLOCK : (half + 1) * BLOCK, :]
            spread = jnp.concatenate([four] * (GROUP // BLOCK), axis=0)
            out_ref[at, cols] = (
                out_ref[at, cols].astype(F32) + jnp.where(mask, spread, 0.0)
            ).astype(BF16)

    for slot in range(2):
        block = jnp.where(lower, theirs[slot][0], mine[slot][0])
        used = jnp.where(lower, theirs[slot][1], mine[slot][1])
        add(block, used, jnp.where(lower, other_ref[slot].astype(F32), own_ref[slot].astype(F32)))
    for slot in range(2):
        add(mine[slot][0], mine[slot][1] & lower, own_ref[slot].astype(F32))


def add_rows(routes, own, other, grad):
    return pl.pallas_call(
        add_kernel,
        out_shape=jax.ShapeDtypeStruct(grad.shape, BF16),
        in_specs=[SMEM_SPEC] * 4 + [VMEM_SPEC] * 3,
        out_specs=VMEM_SPEC,
        compiler_params=pltpu.CompilerParams(vmem_limit_bytes=SMALL_LIMIT),
    )(*routes, own, other, grad)


def on_device(saved, grad_out, route_blocks, route_dest, gain, w_router, w_gate, w_up, w_down):
    sections = lax.axis_size("pipe")
    peers = lax.axis_size("ctx")
    tokens = saved[0]
    model_dim = tokens.shape[1]

    swap = [(i, sections - 1 - i) for i in range(sections)]
    routes = (
        route_blocks,
        route_dest,
        lax.ppermute(route_blocks, "pipe", swap),
        lax.ppermute(route_dest, "pipe", swap),
    )
    kept_rows, handed_rows = pick_blocks(routes, tokens, grad_out)
    pair, gate_w = first_pair(kept_rows, handed_rows, w_gate[0])
    pay, (up_w, down_w) = gather_all(pair, (w_up[0], w_down[0]))
    few = 2 * BLOCK
    run = functools.partial(layer_pass, pay, gain, w_router)
    state, saved_parts = run((gate_w, up_w, down_w), few)
    hidden, normed, active, up_slope, shared_part, shared_x, case = saved_parts

    def corrected(count):
        def branch(state):
            weights = (w_gate[0], w_up[0], w_down[0])
            small = count == few
            if small:
                part, x = shared_part, shared_x
            else:
                part, x = run(weights, count, stream=True)[1][4:6]
            sums, fetched = sum_all(part, weights if small else ())
            upper = shared_rows(x, sums, gain, w_router)
            upper = lax.ppermute(upper, "pipe", swap)
            again = (upper, active, up_slope, hidden)
            return run(fetched if small else weights, few, again, stream=not small)[0]

        return branch

    state = lax.switch(
        case[0], (lambda state: state, corrected(few), corrected(peers * BLOCK)), state
    )
    gate_grad, up_grad, scaled, keep, sent = state

    outers = Outers(((hidden, scaled), (gate_grad, normed), (up_grad, normed)), len(hop_order(peers)))
    sums = scatter_sum(keep.reshape((-1,) + keep.shape[2:]), sent, outers)
    delta, grad_gain, grad_router = delta_rows(kept_rows, handed_rows, sums, gain, w_router)
    other = lax.ppermute(delta, "pipe", swap)
    grad_inputs = add_rows(routes, delta, other, grad_out)
    grad_down, grad_gate, grad_up = outers.results
    return (
        grad_inputs[None],
        grad_gate[None],
        grad_up[None],
        grad_down[None],
        grad_gain,
        grad_router,
    )


def solution(mesh):
    split = P("pipe", "ctx", None)
    row = P("pipe", None)
    return jax.shard_map(
        on_device,
        mesh=mesh,
        in_specs=(split, P("ctx", None), split, split, row, row, split, split, split),
        out_specs=(split, split, split, split, row, row),
        check_vma=False,
    )
```
